32 devices in a mesh: fsdp: 8 (over z, x), rep: 4 (over y, core).
Axes of the slice: x: 2, y: 2, z: 4, core: 2. Of those that a mesh axis runs over, the one named last changes fastest.
Arguments:
- grads: bfloat16 [8, 1024, 768], P('rep', 'fsdp'), may hold values from -6 to 6
- momentum: float32 [8, 1024, 768], P('rep', 'fsdp'), may hold values from -6 to 6
- master: float32 [8, 1024, 768], P('rep', 'fsdp'), may hold values from -0.1875 to 0.1875
- owners: int32 [8], replicated, may hold values from 0 to 7, as said below
- offsets: int32 [8], replicated, may hold values from 0 to 7
Outputs:
- new_momentum: float32 [8, 1024, 768], P('rep', 'fsdp')
- new_master: float32 [8, 1024, 768], P('rep', 'fsdp')
- weights: bfloat16 [8, 1024, 768], P(None, 'fsdp')
- slot_rms: float32 [8, 4], P('fsdp', 'rep')
The draws below stay inside these ranges and needn't reach their ends.
Inputs may be any that keep to these rules, and one draw needn't show every extreme that they name: `owners`: within each aligned block of 2 matrices, no two matrices name the same owner index.
All inputs are finite; a program needn't handle non-finite values.
Results may differ from the reference program's by a relative error of at most 0.0013.
Values may be sent and summed in bfloat16 or wider, within the bound.
No kernel may reach another device: no remote copies, remote signals or barrier semaphores. Data moves between devices by JAX's collectives and lax.ppermute only.
A program may use at most 64 MiB of HBM per device.

```python
import math
import jax
import jax.numpy as jnp
from jax import lax

D = 1024
FF = 768
ITERS = 2
MATS_BLK = 2
MATS = 8
N_FSDP = 8
N_REP = 4


def draw_owners(key, part):
    block_keys = jax.random.split(jax.random.fold_in(key, 17), N_REP)

    def one_block(block_key):
        return jax.random.permutation(block_key, N_FSDP)[:MATS_BLK].astype(jnp.int32)
    return jax.vmap(one_block)(block_keys).reshape(MATS)


def place_ends(entries, rng, smallest, top_value):
    dims = entries.shape
    index_at = [jax.random.randint(jax.random.fold_in(rng, axis), (), 0, dims[axis]) for axis in range(len(dims))]
    entries = entries.at[tuple(index_at)].set(smallest)
    longest = dims.index(max(dims))
    index_at[longest] = (index_at[longest] + 1) % dims[longest]
    return entries.at[tuple(index_at)].set(top_value)


def steps_of(own_key, shape, cuts, smallest, top_value):
    level, own = 1.0, jax.random.fold_in(own_key, 6)
    for dim, shards_of in cuts:
        draws = jnp.exp(jax.random.uniform(jax.random.fold_in(own, dim), (shards_of,), jnp.float32, smallest / len(cuts), top_value / len(cuts)))
        level = level * jnp.repeat(draws, shape[dim] // shards_of).reshape([-1 if axis == dim else 1 for axis in range(len(shape))])
    return level


def centred(key, dims, spread, limit, shards=(), kind=jnp.bfloat16):
    loudness = steps_of(key, dims, shards, -0.22, 0.18) if shards else 1.0
    array = jax.random.normal(key, dims, jnp.float32) * spread * loudness
    return jnp.minimum(jnp.maximum(array, -limit), limit).astype(kind)


def setup_inputs(seed: int = 0) -> dict:
    key_list = jax.random.split(jax.random.key(seed), 6)
    grads = centred(key_list[0], (MATS, D, FF), 1.0, 6.0, ((0, 4), (1, 8)))
    momentum = centred(key_list[1], (MATS, D, FF), 1.0, 6.0, ((0, 4), (1, 8)), jnp.float32)
    master = centred(key_list[2], (MATS, D, FF), D ** -0.5, 0.1875, ((0, 4), (1, 8)), jnp.float32)
    owners = draw_owners(jax.random.fold_in(key_list[5], 71), 0)
    offsets = place_ends(jax.random.randint(key_list[4], (MATS,), 0, N_FSDP), jax.random.fold_in(key_list[4], 1), 0, N_FSDP - 1).astype(jnp.int32)
    return dict(grads=grads, momentum=momentum, master=master, owners=owners, offsets=offsets)


COEF_FIRST = 3.4445
COEF_SECOND = -4.775
COEF_THIRD = 2.0315
MOMENTUM_DECAY = 0.95
LEARN_RATE = 0.02
DECAY_RATE = 0.1
EPSILON = 1e-07

def polish(matrix):
    frobenius = jnp.sqrt(jnp.sum(jnp.square(matrix.astype(jnp.float32))))
    iterate = (matrix.astype(jnp.float32) / (frobenius + EPSILON)).astype(jnp.bfloat16)
    iterate = lax.optimization_barrier(iterate)
    for _ in range(ITERS):
        gram_matrix = lax.dot_general(iterate, iterate, (((0,), (0,)), ((), ())), preferred_element_type=jnp.float32).astype(jnp.bfloat16)
        gram_matrix = lax.optimization_barrier(gram_matrix)
        polynomial = (COEF_SECOND * gram_matrix.astype(jnp.float32) + COEF_THIRD * jnp.dot(gram_matrix, gram_matrix, preferred_element_type=jnp.float32)).astype(jnp.bfloat16)
        iterate = (COEF_FIRST * iterate.astype(jnp.float32) + jnp.dot(iterate, polynomial, preferred_element_type=jnp.float32)).astype(jnp.bfloat16)
        iterate = lax.optimization_barrier(iterate)
    return (iterate, frobenius)

def reference(grads, momentum, master, owners, offsets):
    row_count = D // N_FSDP
    new_momentum = MOMENTUM_DECAY * momentum + grads.astype(jnp.float32)
    half = new_momentum.astype(jnp.bfloat16)

    def polish_one(entry_pair):
        matrix, offset_value = entry_pair
        blocks = matrix.reshape(N_FSDP, row_count, FF)
        ordered = jnp.roll(blocks, offset_value, axis=0).reshape(D, FF)
        iterate, frobenius = polish(ordered)
        stored = jnp.roll(iterate.reshape(N_FSDP, row_count, FF), -offset_value, axis=0).reshape(D, FF)
        return (stored, frobenius)
    polished, norms = lax.map(polish_one, (half, offsets))
    update = 0.2 * math.sqrt(max(D, FF)) * polished.astype(jnp.float32)
    new_master = master - LEARN_RATE * (update + DECAY_RATE * master)
    weight_rows = new_master.astype(jnp.bfloat16)

    def reorder(entry_pair):
        matrix, offset_value = entry_pair
        return jnp.roll(matrix.reshape(N_FSDP, row_count, FF), offset_value, axis=0).reshape(D, FF)
    weights = lax.map(reorder, (weight_rows, offsets))
    positions = jnp.arange(MATS, dtype=jnp.int32)
    block_of = positions // MATS_BLK
    owner_table = (owners[:, None] == jnp.arange(N_FSDP, dtype=jnp.int32)[None, :]).astype(jnp.float32)
    block_table = (block_of[:, None] == jnp.arange(N_REP, dtype=jnp.int32)[None, :]).astype(jnp.float32)
    rms_values = norms / math.sqrt(D * FF)
    slot_rms = jnp.einsum('mo,ms->os', owner_table * rms_values[:, None], block_table)
    return (new_momentum, new_master, weights, slot_rms)
```

```python
import math

import jax
import jax.numpy as jnp
from jax import lax
from jax.sharding import PartitionSpec as P

ITERS = 2


COEF_FIRST = 3.4445
COEF_SECOND = -4.775
COEF_THIRD = 2.0315
MOMENTUM_DECAY = 0.95
LEARN_RATE = 0.02
DECAY_RATE = 0.1
EPSILON = 1e-07
AXES = ("fsdp", "rep")
TAIL = 16


def first_holder(groups):
    return groups // 4


def inward_pairs(step, groups, reps, count):
    steps = groups // 2
    pairs = []
    for f in range(groups):
        for r in range(reps):
            side = r % 2
            place = (f - first_holder(groups) - side) % groups
            i = (place // 2 - step) % steps
            distance = (place - 2 * i) % groups
            if i >= count or distance == 0:
                continue
            holder = (f - distance) % groups
            pairs.append((f * reps + r, holder * reps + r - side + (distance + side) % 2))
    return pairs


def outward_pairs(step, groups, reps, count):
    return [(target, source) for source, target in inward_pairs(step, groups, reps, count)]


def swap(array, groups, reps, bit):
    return lax.ppermute(
        array, AXES, [(f * reps + r, f * reps + (r ^ bit)) for f in range(groups) for r in range(reps)]
    )


def polish(matrix):
    frobenius = jnp.sqrt(jnp.sum(jnp.square(matrix.astype(jnp.float32))))
    iterate = (matrix.astype(jnp.float32) / (frobenius + EPSILON)).astype(jnp.bfloat16)
    iterate = lax.optimization_barrier(iterate)
    for _ in range(ITERS):
        gram_matrix = lax.dot_general(
            iterate, iterate, (((0,), (0,)), ((), ())), preferred_element_type=jnp.float32
        ).astype(jnp.bfloat16)
        gram_matrix = lax.optimization_barrier(gram_matrix)
        polynomial = (
            COEF_SECOND * gram_matrix.astype(jnp.float32)
            + COEF_THIRD * jnp.dot(gram_matrix, gram_matrix, preferred_element_type=jnp.float32)
        ).astype(jnp.bfloat16)
        polynomial = lax.optimization_barrier(polynomial)
        iterate = (
            COEF_FIRST * iterate.astype(jnp.float32)
            + jnp.dot(iterate, polynomial, preferred_element_type=jnp.float32)
        ).astype(jnp.bfloat16)
        iterate = lax.optimization_barrier(iterate)
    return (iterate, frobenius)


def pick(array, index):
    return lax.dynamic_index_in_dim(array, index, 0, keepdims=False)


def on_device(grads, momentum, master, owners, offsets):
    groups, reps = lax.axis_size("fsdp"), lax.axis_size("rep")
    f, r = lax.axis_index("fsdp"), lax.axis_index("rep")
    count, rows, columns = grads.shape
    steps = groups // 2
    side = r % 2
    new_momentum = MOMENTUM_DECAY * momentum + grads.astype(jnp.float32)
    half = new_momentum.astype(jnp.bfloat16)

    place = (f - first_holder(groups) - side) % groups
    held_place = (f - first_holder(groups)) % groups
    held_side = held_place % 2
    held_index = jnp.minimum(held_place // 2, count - 1)
    held_rep = r - side + held_side
    parity = (side + held_side) % 2
    offset = pick(offsets, held_rep * count + held_index)

    def inward(array):
        blocks = []
        for step in range(steps):
            sent = pick(array, jnp.minimum((place // 2 - step) % steps, count - 1))
            blocks.append(lax.ppermute(sent, AXES, inward_pairs(step, groups, reps, count)))
        blocks[0] = jnp.where(parity == 0, pick(array, held_index), blocks[0])
        return jnp.stack(blocks)

    def outward(blocks):
        arrived = [
            lax.ppermute(block, AXES, outward_pairs(step, groups, reps, count))
            for step, block in enumerate(blocks)
        ]
        own = blocks[0]
        arrays = []
        for i in range(count):
            step_of = (place // 2 - i) % steps
            array = arrived[0]
            for step in range(1, steps):
                array = jnp.where(step_of == step, arrived[step], array)
            arrays.append(jnp.where(place == 2 * i, own, array))
        return jnp.stack(arrays)

    mine = inward(half)
    theirs = swap(mine, groups, reps, 1)
    master_mine = inward(master)
    whole = jnp.concatenate([mine, theirs]).reshape(groups * rows, columns)
    iterate, frobenius = polish(whole)
    iterate_mine = iterate.reshape(2, steps, rows, columns)[0]
    scale_factor = 0.2 * math.sqrt(max(groups * rows, columns))

    norm_high = frobenius.astype(jnp.bfloat16)
    norm_rest = lax.optimization_barrier(frobenius - norm_high.astype(jnp.float32))
    norm_middle = norm_rest.astype(jnp.bfloat16)
    norm_low = lax.optimization_barrier(norm_rest - norm_middle.astype(jnp.float32)).astype(jnp.bfloat16)
    lane = lax.broadcasted_iota(jnp.int32, (TAIL, columns), 1)
    tail = jnp.where(lane == 0, norm_high, jnp.where(lane == 1, norm_middle, norm_low))
    returned = outward([jnp.concatenate([iterate_mine[step], tail]) for step in range(steps)])
    update = scale_factor * returned[:, :rows].astype(jnp.float32)
    new_master = master - LEARN_RATE * (update + DECAY_RATE * master)
    norms = jnp.sum(returned[:, rows, :3].astype(jnp.float32), axis=1)

    update_mine = scale_factor * iterate_mine.astype(jnp.float32)
    master_next = master_mine - LEARN_RATE * (update_mine + DECAY_RATE * master_mine)
    weights_mine = master_next.astype(jnp.bfloat16)
    weights_theirs = swap(weights_mine, groups, reps, 1)
    leaving = []
    for step in range(steps):
        distance = (2 * step + parity - offset) % groups
        leaving.append(
            jnp.where(
                distance % 2 == parity,
                pick(weights_mine, distance // 2),
                pick(weights_theirs, distance // 2),
            )
        )
    block_weights = outward(leaving)

    weights = jnp.zeros((reps * count, rows, columns), jnp.bfloat16)
    parts = [(r, block_weights)]
    bit = reps // 2
    while bit:
        parts += [(index ^ bit, swap(part, groups, reps, bit)) for index, part in parts]
        bit //= 2
    for index, part in parts:
        weights = lax.dynamic_update_slice_in_dim(weights, part, index * count, 0)

    block_owners = lax.dynamic_slice_in_dim(owners, r * count, count, 0)
    rms_values = norms / math.sqrt(groups * rows * columns)
    slot_rms = jnp.sum(jnp.where(block_owners == f, rms_values, 0.0)).reshape(1, 1)
    return (new_momentum, new_master, weights, slot_rms)


def solution(mesh):
    in_specs = (P("rep", "fsdp", None), P("rep", "fsdp", None), P("rep", "fsdp", None), P(), P())
    out_specs = (
        P("rep", "fsdp", None),
        P("rep", "fsdp", None),
        P(None, "fsdp", None),
        P("fsdp", "rep"),
    )
    return jax.shard_map(
        on_device, mesh=mesh, in_specs=in_specs, out_specs=out_specs, check_vma=False
    )
```

```python
import functools
import math

import jax
import jax.numpy as jnp
from jax import lax
from jax.experimental import pallas as pl
from jax.experimental.pallas import tpu as pltpu
from jax.sharding import PartitionSpec as P

ITERS = 2


COEF_FIRST = 3.4445
COEF_SECOND = -4.775
COEF_THIRD = 2.0315
MOMENTUM_DECAY = 0.95
LEARN_RATE = 0.02
DECAY_RATE = 0.1
EPSILON = 1e-07
AXES = ("fsdp", "rep")
TAIL = 16
ROWS_OF_TILE = 16
TILE = 256
VMEM_LIMIT = 40 * 2**20
MASTER_TOP = 0.1875
LEAST, SPAN = -125.0, 252.0


def first_place(groups):
    return groups // 4


def step_of(place, i, steps, count):
    return (count - 1 - place // 2) % steps ^ i


def inward_pairs(step, groups, reps, count):
    pairs = []
    for place in range(groups):
        for r in range(reps):
            for i in range(count):
                holder = 2 * i + r % 2
                if holder == place or step_of(place, i, groups // 2, count) != step:
                    continue
                source, target = ((p + first_place(groups)) % groups for p in (place, holder))
                pairs.append((source * reps + r, target * reps + r - r % 2 + place % 2))
    return pairs


def outward_pairs(step, groups, reps, count):
    return [(b, a) for a, b in inward_pairs(step, groups, reps, count)]


def swap(array, groups, reps, bit):
    return lax.ppermute(
        array, AXES, [(f * reps + r, f * reps + (r ^ bit)) for f in range(groups) for r in range(reps)]
    )


def coded(master):
    level = jnp.exp(jnp.log(jnp.abs(master) * (1.0 / MASTER_TOP)) * (1.0 / 3.0))
    size = jnp.exp2(level * SPAN + LEAST)
    return jnp.where(master < 0, -size, size).astype(jnp.bfloat16)


def decoded(code):
    code = code.astype(jnp.float32)
    level = (jnp.log2(jnp.abs(code)) - LEAST) * (1.0 / SPAN)
    size = level * level * level * MASTER_TOP
    return jnp.where(code < 0, -size, size)


def polish_kernel(count, groups, ids, offsets, *refs):
    steps = groups // 2
    blocks, refs = refs[:groups], refs[groups:]
    messages, leaving, scratch = refs[:steps], refs[steps : 2 * steps], refs[2 * steps :]
    iterate, gram, polynomial, code = scratch
    _, rows, columns = blocks[0].shape
    bounds = [(low, min(low + TILE, columns)) for low in range(0, columns, TILE)]
    scale_factor = 0.2 * math.sqrt(max(groups * rows, columns))

    squares = jnp.zeros((8, columns), jnp.float32)
    for block in blocks:
        values = block[0].astype(jnp.float32)
        squares += jnp.sum(jnp.square(values).reshape(rows // 8, 8, columns), axis=0)
    norm = jnp.sqrt(jnp.sum(squares, axis=(0, 1), keepdims=True))
    scale = 1.0 / (norm + EPSILON)
    for index, block in enumerate(blocks):
        iterate[index * rows : (index + 1) * rows] = (block[0].astype(jnp.float32) * scale).astype(
            jnp.bfloat16
        )
        code[index] = block[1]

    def symmetric(out, row_of_tiles):
        for low, high in bounds:
            values = row_of_tiles(low, high).astype(jnp.bfloat16)
            out[low:high, low:] = values
            for other, end in bounds:
                if other > low:
                    out[other:end, low:high] = values[:, other - low : end - low].T

    def gram_tiles(low, high):
        return lax.dot_general(
            iterate[:, low:high],
            iterate[:, low:],
            (((0,), (0,)), ((), ())),
            preferred_element_type=jnp.float32,
        )

    def polynomial_tiles(low, high):
        product = jnp.dot(gram[low:high], gram[:, low:], preferred_element_type=jnp.float32)
        return COEF_SECOND * gram[low:high, low:].astype(jnp.float32) + COEF_THIRD * product

    def next_rows(where):
        values = iterate[where]
        product = jnp.dot(values, polynomial[...], preferred_element_type=jnp.float32)
        return (COEF_FIRST * values.astype(jnp.float32) + product).astype(jnp.bfloat16)

    for iteration in range(ITERS):
        symmetric(gram, gram_tiles)
        symmetric(polynomial, polynomial_tiles)
        if iteration < ITERS - 1:
            for low in range(0, iterate.shape[0], TILE):
                iterate[low : low + TILE] = next_rows(slice(low, low + TILE))

    f, r = ids[0], ids[1]
    side = lax.rem(r, 2)
    place = lax.rem(f - first_place(groups) + groups, groups)
    held = jnp.minimum(lax.div(place, 2), count - 1)
    offset = offsets[(r - side + lax.rem(place, 2)) * count + held]
    for step in range(steps):
        target = 2 * lax.rem(count - 1 - (step ^ held) + steps, steps) + side
        source = lax.rem(target - offset + groups, groups)
        index = lax.rem(count - 1 - lax.div(source, 2) + steps, steps) ^ held
        index += jnp.where(lax.rem(source, 2) == side, 0, steps)
        start = pl.multiple_of(index * rows, rows)
        update = scale_factor * next_rows(pl.ds(start, rows)).astype(jnp.float32)
        master = decoded(code[index])
        leaving[step][...] = (master - LEARN_RATE * (update + DECAY_RATE * master)).astype(jnp.bfloat16)

    high = norm.astype(jnp.bfloat16).astype(jnp.float32)
    middle = (norm - high).astype(jnp.bfloat16).astype(jnp.float32)
    lane = lax.broadcasted_iota(jnp.int32, (TAIL, columns), 1)
    tail = jnp.where(lane == 0, high, jnp.where(lane == 1, middle, norm - high - middle))
    for index, message in enumerate(messages):
        message[:rows] = next_rows(slice(index * rows, (index + 1) * rows))
        message[rows:] = tail.astype(jnp.bfloat16)


def polish_plain(f, r, offsets, count, groups, blocks):
    _, rows, columns = blocks[0].shape
    steps = groups // 2
    side = r % 2
    place = (f - first_place(groups)) % groups
    held = jnp.minimum(place // 2, count - 1)
    offset = pick(offsets, (r - side + place % 2) * count + held)
    blocks = jnp.stack(blocks)
    matrix = blocks[:, 0].reshape(groups * rows, columns).astype(jnp.float32)
    norm = jnp.sqrt(jnp.sum(jnp.square(matrix)))
    iterate = lax.optimization_barrier((matrix / (norm + EPSILON)).astype(jnp.bfloat16))
    for _ in range(ITERS):
        gram = lax.dot_general(
            iterate, iterate, (((0,), (0,)), ((), ())), preferred_element_type=jnp.float32
        ).astype(jnp.bfloat16)
        product = jnp.dot(gram, gram, preferred_element_type=jnp.float32)
        polynomial = COEF_SECOND * gram.astype(jnp.float32) + COEF_THIRD * product
        product = jnp.dot(iterate, polynomial.astype(jnp.bfloat16), preferred_element_type=jnp.float32)
        iterate = (COEF_FIRST * iterate.astype(jnp.float32) + product).astype(jnp.bfloat16)
        iterate = lax.optimization_barrier(iterate)
    iterate = iterate.reshape(groups, rows, columns)
    update = 0.2 * math.sqrt(max(groups * rows, columns)) * iterate.astype(jnp.float32)
    master = decoded(blocks[:, 1])
    weights = (master - LEARN_RATE * (update + DECAY_RATE * master)).astype(jnp.bfloat16)
    leaving = []
    for step in range(steps):
        source = (2 * ((count - 1 - (step ^ held)) % steps) + side - offset) % groups
        index = (count - 1 - source // 2) % steps ^ held
        leaving.append(pick(weights, index + jnp.where(source % 2 == side, 0, steps)))
    high = norm.astype(jnp.bfloat16)
    rest = lax.optimization_barrier(norm - high.astype(jnp.float32))
    middle = rest.astype(jnp.bfloat16)
    low = lax.optimization_barrier(rest - middle.astype(jnp.float32)).astype(jnp.bfloat16)
    lane = lax.broadcasted_iota(jnp.int32, (TAIL, columns), 1)
    tail = jnp.where(lane == 0, high, jnp.where(lane == 1, middle, low))
    return [jnp.concatenate([iterate[step], tail]) for step in range(steps)], leaving


def polish(f, r, offsets, count, groups, blocks):
    _, rows, columns = blocks[0].shape
    if rows % ROWS_OF_TILE:
        return polish_plain(f, r, offsets, count, groups, blocks)
    steps = groups // 2
    in_vmem = pl.BlockSpec(memory_space=pltpu.VMEM)
    square = pltpu.VMEM((columns, columns), jnp.bfloat16)
    results = pl.pallas_call(
        functools.partial(polish_kernel, count, groups),
        out_shape=[jax.ShapeDtypeStruct((rows + TAIL, columns), jnp.bfloat16)] * steps
        + [jax.ShapeDtypeStruct((rows, columns), jnp.bfloat16)] * steps,
        in_specs=[pl.BlockSpec(memory_space=pltpu.SMEM)] * 2 + [in_vmem] * groups,
        out_specs=[in_vmem] * groups,
        scratch_shapes=[
            pltpu.VMEM((groups * rows, columns), jnp.bfloat16),
            square,
            square,
            pltpu.VMEM((groups, rows, columns), jnp.bfloat16),
        ],
        compiler_params=pltpu.CompilerParams(vmem_limit_bytes=VMEM_LIMIT),
    )(jnp.stack([f, r]), offsets, *blocks)
    return results[:steps], results[steps:]


def apply_kernel(count, groups, reps, ids, owners, master, *refs):
    steps = groups // 2
    returned, messages, refs = refs[:steps], refs[steps : 2 * steps], refs[2 * steps :]
    parts, (new_master, weights, slot_rms, semaphores) = refs[:reps], refs[reps:]
    _, rows, columns = master.shape
    scale_factor = 0.2 * math.sqrt(max(groups * rows, columns))
    f, r = ids[0], ids[1]
    place = lax.rem(f - first_place(groups) + groups, groups)
    half_place = lax.div(place, 2)
    turn = lax.rem(lax.rem(count - 1 - half_place + steps, steps), count)
    copies = []
    for other, part in enumerate(parts):
        for j in range(count):
            matrix = (r ^ other) * count + (turn ^ j)
            copies.append(pltpu.make_async_copy(part.at[j], weights.at[matrix], semaphores.at[other * count + j]))
            copies[-1].start()
    own = lax.rem(r, 2) == lax.rem(place, 2)
    slot_rms[...] = jnp.zeros((1, 1), jnp.float32)

    def take(i, message):
        update = scale_factor * message[:rows].astype(jnp.float32)
        new_master[i] = master[i] - LEARN_RATE * (update + DECAY_RATE * master[i])
        shape = (TAIL, columns)
        row, lane = (lax.broadcasted_iota(jnp.int32, shape, n) for n in (0, 1))
        norm = jnp.where((row == 0) & (lane < 3), message[rows:].astype(jnp.float32), 0.0)
        norm = jnp.sum(norm, axis=(0, 1), keepdims=True)
        here = owners[r * count + i] == f
        slot_rms[...] += jnp.where(here, norm * (1.0 / math.sqrt(groups * rows * columns)), 0.0)

    for i in range(count):
        arrival = lax.rem(count - 1 - half_place + steps, steps) ^ i
        held = own & (half_place == i)
        for step in range(steps):

            @pl.when((arrival == step) & jnp.logical_not(held))
            def _():
                take(i, returned[step])

            if step_of(2 * i, i, steps, count) == step:

                @pl.when(held)
                def _():
                    take(i, messages[step])

    for copy in copies:
        copy.wait()


def apply_plain(f, r, owners, count, groups, reps, master, returned, messages, parts):
    _, rows, columns = master.shape
    steps = groups // 2
    place = (f - first_place(groups)) % groups
    half_place = place // 2
    own = r % 2 == place % 2
    order = (count - 1 - half_place) % steps
    returned, messages = jnp.stack(returned), jnp.stack(messages)
    new_master, slot_rms = [], jnp.zeros((1, 1), jnp.float32)
    for i in range(count):
        message = jnp.where(own & (half_place == i), pick(messages, order ^ i), pick(returned, order ^ i))
        update = 0.2 * math.sqrt(max(groups * rows, columns)) * message[:rows].astype(jnp.float32)
        new_master.append(master[i] - LEARN_RATE * (update + DECAY_RATE * master[i]))
        rms = jnp.sum(message[rows, :3].astype(jnp.float32)) / math.sqrt(groups * rows * columns)
        slot_rms += jnp.where(pick(owners, r * count + i) == f, rms, 0.0)
    weights = jnp.zeros((reps * count, rows, columns), jnp.bfloat16)
    for other, part in enumerate(parts):
        for j in range(count):
            index = (r ^ other) * count + (order % count ^ j)
            weights = lax.dynamic_update_slice_in_dim(weights, part[j : j + 1], index, 0)
    return jnp.stack(new_master), weights, slot_rms


def apply(f, r, owners, count, groups, reps, master, returned, messages, parts):
    in_vmem = pl.BlockSpec(memory_space=pltpu.VMEM)
    in_smem = pl.BlockSpec(memory_space=pltpu.SMEM)
    _, rows, columns = master.shape
    if rows % ROWS_OF_TILE:
        return apply_plain(f, r, owners, count, groups, reps, master, returned, messages, parts)
    return pl.pallas_call(
        functools.partial(apply_kernel, count, groups, reps),
        out_shape=[
            jax.ShapeDtypeStruct(master.shape, jnp.float32),
            jax.ShapeDtypeStruct((reps * count, rows, columns), jnp.bfloat16),
            jax.ShapeDtypeStruct((1, 1), jnp.float32),
        ],
        in_specs=[in_smem] * 2 + [in_vmem] * (1 + 2 * len(messages) + reps),
        out_specs=[in_vmem, pl.BlockSpec(memory_space=pl.ANY), in_vmem],
        scratch_shapes=[pltpu.SemaphoreType.DMA((reps * count,))],
        compiler_params=pltpu.CompilerParams(vmem_limit_bytes=VMEM_LIMIT),
    )(jnp.stack([f, r]), owners, master, *returned, *messages, *parts)


def pick(array, index):
    return lax.dynamic_index_in_dim(array, index, 0, keepdims=False)


def on_device(grads, momentum, master, owners, offsets):
    groups, reps = lax.axis_size("fsdp"), lax.axis_size("rep")
    f, r = lax.axis_index("fsdp"), lax.axis_index("rep")
    count, rows, columns = grads.shape
    steps = groups // 2
    scale_factor = 0.2 * math.sqrt(max(groups * rows, columns))
    side = r % 2
    place = (f - first_place(groups)) % groups
    half_place = place // 2
    held = jnp.minimum(half_place, count - 1)
    holds_own = (side == place % 2) & (half_place < count)

    turn = (count - 1 - half_place) % steps % count
    own_step = step_of(2 * held, held, steps, count)

    def inward_sends(array_of, chosen):
        return {
            step: lax.ppermute(
                array_of(step % count), AXES, inward_pairs(step, groups, reps, count)
            )
            for step in chosen
        }

    def with_own(step, block, own):
        return jnp.where(holds_own & (own_step == step), own, block)

    def half_of(i):
        return (MOMENTUM_DECAY * pick(momentum, i) + pick(grads, i).astype(jnp.float32)).astype(
            jnp.bfloat16
        )

    sent = lax.optimization_barrier(
        [jnp.stack([half_of(j ^ turn), coded(pick(master, j ^ turn))]) for j in range(count)]
    )
    blocks = inward_sends(lambda j: sent[j], range(steps))
    new_momentum = MOMENTUM_DECAY * momentum + grads.astype(jnp.float32)

    def own_of(arrays):
        own = arrays[0]
        for j in range(1, count):
            own = jnp.where((held ^ turn) == j, arrays[j], own)
        return own

    def both_sides(blocks, own):
        mine = [with_own(step, blocks[step], own) for step in range(steps)]
        return mine + [swap(block, groups, reps, 1) for block in mine]

    blocks = both_sides(blocks, own_of(sent))
    blocks, new_momentum = lax.optimization_barrier((blocks, new_momentum))
    messages, leaving = polish(f, r, offsets, count, groups, blocks)
    kept = messages
    arrived = [
        lax.ppermute(block, AXES, outward_pairs(step, groups, reps, count))
        for step, block in enumerate(leaving)
    ]

    part = []
    for j in range(count):
        rows_in = arrived[j]
        for step in range(j + count, steps, count):
            rows_in = jnp.where((count - 1 - half_place) % steps // count * count + j == step, arrived[step], rows_in)
        for step in sorted({step_of(2 * i, i, steps, count) for i in range(count)}):
            if step % count == j:
                rows_in = with_own(step, rows_in, leaving[step])
        part.append(rows_in)
    part, messages = lax.optimization_barrier((jnp.stack(part), messages))
    returned = [
        lax.ppermute(message, AXES, outward_pairs(step, groups, reps, count))
        for step, message in enumerate(messages)
    ]

    parts = [part] + [None] * (reps - 1)
    bit = reps // 2
    while bit:
        for other in range(0, reps, 2 * bit):
            parts[other ^ bit] = swap(parts[other], groups, reps, bit)
        if bit == reps // 2:
            parts, returned = lax.optimization_barrier((parts, returned))
        bit //= 2
    new_master, weights, slot_rms = apply(
        f, r, owners, count, groups, reps, master, returned, kept, parts
    )
    return (new_momentum, new_master, weights, slot_rms)


def solution(mesh):
    in_specs = (P("rep", "fsdp", None), P("rep", "fsdp", None), P("rep", "fsdp", None), P(), P())
    out_specs = (
        P("rep", "fsdp", None),
        P("rep", "fsdp", None),
        P(None, "fsdp", None),
        P("fsdp", "rep"),
    )
    return jax.shard_map(
        on_device, mesh=mesh, in_specs=in_specs, out_specs=out_specs, check_vma=False
    )
```

```python
import functools
import math

import jax
import jax.numpy as jnp
from jax import lax
from jax.experimental import pallas as pl
from jax.experimental.pallas import tpu as pltpu
from jax.sharding import PartitionSpec as P

ITERS = 2


COEF_FIRST = 3.4445
COEF_SECOND = -4.775
COEF_THIRD = 2.0315
MOMENTUM_DECAY = 0.95
LEARN_RATE = 0.02
DECAY_RATE = 0.1
EPSILON = 1e-07
AXES = ("fsdp", "rep")
TAIL = 16
ROWS_OF_TILE = 16
TILE = 256
VMEM_LIMIT = 40 * 2**20
MASTER_TOP = 0.1875
LEAST, SPAN = -125.0, 252.0


def first_place(groups):
    return groups // 4


def step_of(place, i, steps, count):
    return place // 2 ^ i


def inward_pairs(step, groups, reps, count):
    pairs = []
    for place in range(groups):
        for r in range(reps):
            for i in range(count):
                holder = 2 * i + r % 2
                if holder == place or step_of(place, i, groups // 2, count) != step:
                    continue
                source, target = ((p + first_place(groups)) % groups for p in (place, holder))
                pairs.append((source * reps + r, target * reps + r - r % 2 + place % 2))
    return pairs


def outward_pairs(step, groups, reps, count):
    return [(b, a) for a, b in inward_pairs(step, groups, reps, count)]


def swap(array, groups, reps, bit):
    return lax.ppermute(
        array, AXES, [(f * reps + r, f * reps + (r ^ bit)) for f in range(groups) for r in range(reps)]
    )


def coded(master):
    level = jnp.exp(jnp.log(jnp.abs(master) * (1.0 / MASTER_TOP)) * (1.0 / 3.0))
    size = jnp.exp2(level * SPAN + LEAST)
    return jnp.where(master < 0, -size, size).astype(jnp.bfloat16)


def decoded(code):
    code = code.astype(jnp.float32)
    level = (jnp.log2(jnp.abs(code)) - LEAST) * (1.0 / SPAN)
    size = level * level * level * MASTER_TOP
    return jnp.where(code < 0, -size, size)


def polish_kernel(count, groups, ids, offsets, *refs):
    steps = groups // 2
    blocks, refs = refs[:groups], refs[groups:]
    messages, leaving, scratch = refs[:steps], refs[steps : 2 * steps], refs[2 * steps :]
    iterate, gram, polynomial, code = scratch
    _, rows, columns = blocks[0].shape
    bounds = [(low, min(low + TILE, columns)) for low in range(0, columns, TILE)]
    scale_factor = 0.2 * math.sqrt(max(groups * rows, columns))

    for index, block in enumerate(blocks):
        iterate[index * rows : (index + 1) * rows] = block[0]
        code[index] = block[1]

    def symmetric(out, row_of_tiles):
        for low, high in bounds:
            values = row_of_tiles(low, high).astype(jnp.bfloat16)
            out[low:high, low:] = values
            for other, end in bounds:
                if other > low:
                    out[other:end, low:high] = values[:, other - low : end - low].T

    def gram_tiles(low, high):
        return lax.dot_general(
            iterate[:, low:high],
            iterate[:, low:],
            (((0,), (0,)), ((), ())),
            preferred_element_type=jnp.float32,
        )

    traces = []

    def raw_tiles(low, high):
        values = gram_tiles(low, high)
        shape = (high - low, high - low)
        row, lane = (lax.broadcasted_iota(jnp.int32, shape, n) for n in (0, 1))
        diagonal = jnp.where(row == lane, values[:, : high - low], 0.0)
        traces.append(jnp.sum(diagonal, axis=(0, 1), keepdims=True))
        return values

    def polynomial_tiles(factor, low, high):
        product = jnp.dot(gram[low:high], gram[:, low:], preferred_element_type=jnp.float32)
        first = (COEF_SECOND * factor) * gram[low:high, low:].astype(jnp.float32)
        return first + (COEF_THIRD * factor * factor) * product

    def next_rows(values):
        product = jnp.dot(values, polynomial[...], preferred_element_type=jnp.float32)
        return (COEF_FIRST * values.astype(jnp.float32) + product).astype(jnp.bfloat16)

    symmetric(gram, raw_tiles)
    norm = jnp.sqrt(sum(traces))
    scale = 1.0 / (norm + EPSILON)
    symmetric(polynomial, functools.partial(polynomial_tiles, scale * scale))
    for low in range(0, iterate.shape[0], TILE):
        values = iterate[low : low + TILE].astype(jnp.float32) * scale
        iterate[low : low + TILE] = next_rows(values.astype(jnp.bfloat16))
    for iteration in range(1, ITERS):
        symmetric(gram, gram_tiles)
        symmetric(polynomial, functools.partial(polynomial_tiles, 1.0))
        if iteration < ITERS - 1:
            for low in range(0, iterate.shape[0], TILE):
                iterate[low : low + TILE] = next_rows(iterate[low : low + TILE])

    f, r = ids[0], ids[1]
    side = lax.rem(r, 2)
    place = lax.rem(f - first_place(groups) + groups, groups)
    held = jnp.minimum(lax.div(place, 2), count - 1)
    offset = offsets[(r - side + lax.rem(place, 2)) * count + held]
    for step in range(steps):
        target = 2 * (step ^ held) + side
        source = lax.rem(target - offset + groups, groups)
        index = lax.div(source, 2) ^ held
        index += jnp.where(lax.rem(source, 2) == side, 0, steps)
        start = pl.multiple_of(index * rows, rows)
        update = scale_factor * next_rows(iterate[pl.ds(start, rows)]).astype(jnp.float32)
        master = decoded(code[index])
        leaving[step][...] = (master - LEARN_RATE * (update + DECAY_RATE * master)).astype(jnp.bfloat16)

    high = norm.astype(jnp.bfloat16).astype(jnp.float32)
    middle = (norm - high).astype(jnp.bfloat16).astype(jnp.float32)
    lane = lax.broadcasted_iota(jnp.int32, (TAIL, columns), 1)
    tail = jnp.where(lane == 0, high, jnp.where(lane == 1, middle, norm - high - middle))
    for index, message in enumerate(messages):
        message[:rows] = next_rows(iterate[index * rows : (index + 1) * rows])
        message[rows:] = tail.astype(jnp.bfloat16)


def polish_plain(f, r, offsets, count, groups, blocks):
    _, rows, columns = blocks[0].shape
    steps = groups // 2
    side = r % 2
    place = (f - first_place(groups)) % groups
    held = jnp.minimum(place // 2, count - 1)
    offset = pick(offsets, (r - side + place % 2) * count + held)
    blocks = jnp.stack(blocks)
    matrix = blocks[:, 0].reshape(groups * rows, columns).astype(jnp.float32)
    norm = jnp.sqrt(jnp.sum(jnp.square(matrix)))
    iterate = lax.optimization_barrier((matrix / (norm + EPSILON)).astype(jnp.bfloat16))
    for _ in range(ITERS):
        gram = lax.dot_general(
            iterate, iterate, (((0,), (0,)), ((), ())), preferred_element_type=jnp.float32
        ).astype(jnp.bfloat16)
        product = jnp.dot(gram, gram, preferred_element_type=jnp.float32)
        polynomial = COEF_SECOND * gram.astype(jnp.float32) + COEF_THIRD * product
        product = jnp.dot(iterate, polynomial.astype(jnp.bfloat16), preferred_element_type=jnp.float32)
        iterate = (COEF_FIRST * iterate.astype(jnp.float32) + product).astype(jnp.bfloat16)
        iterate = lax.optimization_barrier(iterate)
    iterate = iterate.reshape(groups, rows, columns)
    update = 0.2 * math.sqrt(max(groups * rows, columns)) * iterate.astype(jnp.float32)
    master = decoded(blocks[:, 1])
    weights = (master - LEARN_RATE * (update + DECAY_RATE * master)).astype(jnp.bfloat16)
    leaving = []
    for step in range(steps):
        source = (2 * (step ^ held) + side - offset) % groups
        index = source // 2 ^ held
        leaving.append(pick(weights, index + jnp.where(source % 2 == side, 0, steps)))
    high = norm.astype(jnp.bfloat16)
    rest = lax.optimization_barrier(norm - high.astype(jnp.float32))
    middle = rest.astype(jnp.bfloat16)
    low = lax.optimization_barrier(rest - middle.astype(jnp.float32)).astype(jnp.bfloat16)
    lane = lax.broadcasted_iota(jnp.int32, (TAIL, columns), 1)
    tail = jnp.where(lane == 0, high, jnp.where(lane == 1, middle, low))
    return [jnp.concatenate([iterate[step], tail]) for step in range(steps)], leaving


def polish(ids, offsets, count, groups, blocks):
    _, rows, columns = blocks[0].shape
    if rows % ROWS_OF_TILE:
        return polish_plain(*ids, offsets, count, groups, blocks)
    steps = groups // 2
    in_vmem = pl.BlockSpec(memory_space=pltpu.VMEM)
    square = pltpu.VMEM((columns, columns), jnp.bfloat16)
    results = pl.pallas_call(
        functools.partial(polish_kernel, count, groups),
        out_shape=[jax.ShapeDtypeStruct((rows + TAIL, columns), jnp.bfloat16)] * steps
        + [jax.ShapeDtypeStruct((rows, columns), jnp.bfloat16)] * steps,
        in_specs=[pl.BlockSpec(memory_space=pltpu.SMEM)] * 2 + [in_vmem] * groups,
        out_specs=[in_vmem] * groups,
        scratch_shapes=[
            pltpu.VMEM((groups * rows, columns), jnp.bfloat16),
            square,
            square,
            pltpu.VMEM((groups, rows, columns), jnp.bfloat16),
        ],
        compiler_params=pltpu.CompilerParams(vmem_limit_bytes=VMEM_LIMIT),
    )(ids, offsets, *blocks)
    return results[:steps], results[steps:]


def apply_kernel(count, groups, reps, ids, owners, master, *refs):
    steps = groups // 2
    returned, messages, refs = refs[:steps], refs[steps : 2 * steps], refs[2 * steps :]
    parts, (new_master, weights, slot_rms, semaphores) = refs[: reps * count], refs[reps * count :]
    _, rows, columns = master.shape
    scale_factor = 0.2 * math.sqrt(max(groups * rows, columns))
    f, r = ids[0], ids[1]
    place = lax.rem(f - first_place(groups) + groups, groups)
    half_place = lax.div(place, 2)
    turn = lax.rem(half_place, count)
    copies = []
    for n, part in enumerate(parts):
        matrix = (r ^ n // count) * count + (turn ^ n % count)
        copies.append(pltpu.make_async_copy(part, weights.at[matrix], semaphores.at[n]))
        copies[-1].start()
    own = lax.rem(r, 2) == lax.rem(place, 2)
    slot_rms[...] = jnp.zeros((1, 1), jnp.float32)

    def take(i, message):
        update = scale_factor * message[:rows].astype(jnp.float32)
        new_master[i] = master[i] - LEARN_RATE * (update + DECAY_RATE * master[i])
        shape = (TAIL, columns)
        row, lane = (lax.broadcasted_iota(jnp.int32, shape, n) for n in (0, 1))
        norm = jnp.where((row == 0) & (lane < 3), message[rows:].astype(jnp.float32), 0.0)
        norm = jnp.sum(norm, axis=(0, 1), keepdims=True)
        here = owners[r * count + i] == f
        slot_rms[...] += jnp.where(here, norm * (1.0 / math.sqrt(groups * rows * columns)), 0.0)

    for i in range(count):
        arrival = half_place ^ i
        held = own & (half_place == i)
        for step in range(steps):

            @pl.when((arrival == step) & jnp.logical_not(held))
            def _():
                take(i, returned[steps - 1 - step])

            if step_of(2 * i, i, steps, count) == step:

                @pl.when(held)
                def _():
                    take(i, messages[step])

    for copy in copies:
        copy.wait()


def apply_plain(f, r, owners, count, groups, reps, master, returned, messages, parts):
    _, rows, columns = master.shape
    steps = groups // 2
    place = (f - first_place(groups)) % groups
    half_place = place // 2
    own = r % 2 == place % 2
    order = half_place
    returned, messages = jnp.stack(returned), jnp.stack(messages)
    new_master, slot_rms = [], jnp.zeros((1, 1), jnp.float32)
    for i in range(count):
        message = jnp.where(own & (half_place == i), pick(messages, order ^ i), pick(returned, order ^ i))
        update = 0.2 * math.sqrt(max(groups * rows, columns)) * message[:rows].astype(jnp.float32)
        new_master.append(master[i] - LEARN_RATE * (update + DECAY_RATE * master[i]))
        rms = jnp.sum(message[rows, :3].astype(jnp.float32)) / math.sqrt(groups * rows * columns)
        slot_rms += jnp.where(pick(owners, r * count + i) == f, rms, 0.0)
    weights = jnp.zeros((reps * count, rows, columns), jnp.bfloat16)
    for other, part in enumerate(parts):
        for j in range(count):
            index = (r ^ other) * count + (order % count ^ j)
            weights = lax.dynamic_update_slice_in_dim(weights, part[j][None], index, 0)
    return jnp.stack(new_master), weights, slot_rms


def apply(ids, owners, count, groups, reps, master, returned, messages, parts):
    in_vmem = pl.BlockSpec(memory_space=pltpu.VMEM)
    in_smem = pl.BlockSpec(memory_space=pltpu.SMEM)
    _, rows, columns = master.shape
    if rows % ROWS_OF_TILE:
        return apply_plain(*ids, owners, count, groups, reps, master, returned, messages, parts)
    return pl.pallas_call(
        functools.partial(apply_kernel, count, groups, reps),
        out_shape=[
            jax.ShapeDtypeStruct(master.shape, jnp.float32),
            jax.ShapeDtypeStruct((reps * count, rows, columns), jnp.bfloat16),
            jax.ShapeDtypeStruct((1, 1), jnp.float32),
        ],
        in_specs=[in_smem] * 2 + [in_vmem] * (1 + 2 * len(messages) + reps * count),
        out_specs=[in_vmem, pl.BlockSpec(memory_space=pl.ANY), in_vmem],
        scratch_shapes=[pltpu.SemaphoreType.DMA((reps * count,))],
        compiler_params=pltpu.CompilerParams(vmem_limit_bytes=VMEM_LIMIT),
    )(ids, owners, master, *returned[::-1], *messages, *(one for part in parts for one in part))


def pick(array, index):
    return lax.dynamic_index_in_dim(array, index, 0, keepdims=False)


def on_device(grads, momentum, master, owners, offsets):
    groups, reps = lax.axis_size("fsdp"), lax.axis_size("rep")
    f, r = lax.axis_index("fsdp"), lax.axis_index("rep")
    count, rows, columns = grads.shape
    steps = groups // 2
    scale_factor = 0.2 * math.sqrt(max(groups * rows, columns))
    ids = jnp.stack([f, r])
    side = r % 2
    place = (f - first_place(groups)) % groups
    half_place = place // 2
    held = jnp.minimum(half_place, count - 1)
    holds_own = (side == place % 2) & (half_place < count)

    turn = half_place % count
    own_step = step_of(2 * held, held, steps, count)

    def inward_sends(array_of, chosen):
        return {
            step: lax.ppermute(
                array_of(step % count), AXES, inward_pairs(step, groups, reps, count)
            )
            for step in chosen
        }

    def with_own(step, block, own):
        return jnp.where(holds_own & (own_step == step), own, block)

    def half_of(i):
        return (MOMENTUM_DECAY * pick(momentum, i) + pick(grads, i).astype(jnp.float32)).astype(
            jnp.bfloat16
        )

    sent = lax.optimization_barrier(
        [jnp.stack([half_of(j ^ turn), coded(pick(master, j ^ turn))]) for j in range(count)]
    )
    blocks = inward_sends(lambda j: sent[j], range(steps))
    new_momentum = MOMENTUM_DECAY * momentum + grads.astype(jnp.float32)

    blocks[steps - 1], new_momentum = lax.optimization_barrier((blocks[steps - 1], new_momentum))

    def own_of(arrays):
        own = arrays[0]
        for j in range(1, count):
            own = jnp.where((held ^ turn) == j, arrays[j], own)
        return own

    def both_sides(blocks, own):
        mine = [with_own(step, blocks[step], own) for step in range(steps)]
        return mine + [swap(block, groups, reps, 1) for block in mine]

    blocks = both_sides(blocks, own_of(sent))
    messages, leaving = polish(ids, offsets, count, groups, blocks)
    kept = messages

    def outward(blocks):
        return [
            lax.ppermute(block, AXES, outward_pairs(step, groups, reps, count))
            for step, block in reversed([*enumerate(blocks)])
        ][::-1]

    arrived = lax.optimization_barrier(outward(leaving)[::-1])[::-1]

    part = []
    for j in range(count):
        rows_in = arrived[j]
        for step in range(j + count, steps, count):
            rows_in = jnp.where(half_place // count * count + j == step, arrived[step], rows_in)
        for step in sorted({step_of(2 * i, i, steps, count) for i in range(count)}):
            if step % count == j:
                rows_in = with_own(step, rows_in, leaving[step])
        part.append(rows_in)
    returned = outward(messages)

    parts = [part] + [None] * (reps - 1)
    bit = reps // 2
    while bit:
        for other in range(0, reps, 2 * bit):
            parts[other ^ bit] = [swap(one, groups, reps, bit) for one in parts[other]]
        bit //= 2
    new_master, weights, slot_rms = apply(
        ids, owners, count, groups, reps, master, returned, kept, parts
    )
    return (new_momentum, new_master, weights, slot_rms)


def solution(mesh):
    in_specs = (P("rep", "fsdp", None), P("rep", "fsdp", None), P("rep", "fsdp", None), P(), P())
    out_specs = (
        P("rep", "fsdp", None),
        P("rep", "fsdp", None),
        P(None, "fsdp", None),
        P("fsdp", "rep"),
    )
    return jax.shard_map(
        on_device, mesh=mesh, in_specs=in_specs, out_specs=out_specs, check_vma=False
    )
```

```python
import functools
import math

import jax
import jax.numpy as jnp
from jax import lax
from jax.experimental import pallas as pl
from jax.experimental.pallas import tpu as pltpu
from jax.sharding import PartitionSpec as P

ITERS = 2


COEF_FIRST = 3.4445
COEF_SECOND = -4.775
COEF_THIRD = 2.0315
MOMENTUM_DECAY = 0.95
LEARN_RATE = 0.02
DECAY_RATE = 0.1
EPSILON = 1e-07
AXES = ("fsdp", "rep")
TAIL = 16
ROWS_OF_TILE = 16
TILE = 256
VMEM_LIMIT = 40 * 2**20
MASTER_TOP = 0.1875
LEAST, SPAN = -125.0, 252.0


def first_place(groups):
    return groups // 4


def step_of(place, i, steps, count):
    return place // 2 ^ i


def inward_pairs(step, groups, reps, count):
    pairs = []
    for place in range(groups):
        for r in range(reps):
            for i in range(count):
                holder = 2 * i + r % 2
                if holder == place or step_of(place, i, groups // 2, count) != step:
                    continue
                source, target = ((p + first_place(groups)) % groups for p in (place, holder))
                pairs.append((source * reps + r, target * reps + r - r % 2 + place % 2))
    return pairs


def outward_pairs(step, groups, reps, count):
    return [(b, a) for a, b in inward_pairs(step, groups, reps, count)]


def swap(array, groups, reps, bit):
    return lax.ppermute(
        array, AXES, [(f * reps + r, f * reps + (r ^ bit)) for f in range(groups) for r in range(reps)]
    )


def coded(master):
    level = jnp.exp(jnp.log(jnp.abs(master) * (1.0 / MASTER_TOP)) * (1.0 / 3.0))
    size = jnp.exp2(level * SPAN + LEAST)
    return jnp.where(master < 0, -size, size).astype(jnp.bfloat16)


def decoded(code):
    code = code.astype(jnp.float32)
    level = (jnp.log2(jnp.abs(code)) - LEAST) * (1.0 / SPAN)
    size = level * level * level * MASTER_TOP
    return jnp.where(code < 0, -size, size)


def polish_kernel(count, groups, ids, offsets, *refs):
    steps = groups // 2
    blocks, refs = refs[:groups], refs[groups:]
    messages, leaving, scratch = refs[:steps], refs[steps : 2 * steps], refs[2 * steps :]
    iterate, gram, polynomial, code = scratch
    _, rows, columns = blocks[0].shape
    bounds = [(low, min(low + TILE, columns)) for low in range(0, columns, TILE)]
    scale_factor = 0.2 * math.sqrt(max(groups * rows, columns))

    for index, block in enumerate(blocks):
        iterate[index * rows : (index + 1) * rows] = block[0]
        code[index] = block[1]

    def symmetric(out, row_of_tiles):
        for low, high in bounds:
            values = row_of_tiles(low, high).astype(jnp.bfloat16)
            out[low:high, low:] = values
            for other, end in bounds:
                if other > low:
                    out[other:end, low:high] = values[:, other - low : end - low].T

    def gram_tiles(low, high):
        return lax.dot_general(
            iterate[:, low:high],
            iterate[:, low:],
            (((0,), (0,)), ((), ())),
            preferred_element_type=jnp.float32,
        )

    traces = []

    def raw_tiles(low, high):
        values = gram_tiles(low, high)
        shape = (high - low, high - low)
        row, lane = (lax.broadcasted_iota(jnp.int32, shape, n) for n in (0, 1))
        diagonal = jnp.where(row == lane, values[:, : high - low], 0.0)
        traces.append(jnp.sum(diagonal, axis=(0, 1), keepdims=True))
        return values

    def polynomial_tiles(factor, low, high):
        product = jnp.dot(gram[low:high], gram[:, low:], preferred_element_type=jnp.float32)
        first = (COEF_SECOND * factor) * gram[low:high, low:].astype(jnp.float32)
        return first + (COEF_THIRD * factor * factor) * product

    def next_rows(values):
        product = jnp.dot(values, polynomial[...], preferred_element_type=jnp.float32)
        return (COEF_FIRST * values.astype(jnp.float32) + product).astype(jnp.bfloat16)

    symmetric(gram, raw_tiles)
    norm = jnp.sqrt(sum(traces))
    scale = 1.0 / (norm + EPSILON)
    symmetric(polynomial, functools.partial(polynomial_tiles, scale * scale))
    for low in range(0, iterate.shape[0], TILE):
        values = iterate[low : low + TILE].astype(jnp.float32) * scale
        iterate[low : low + TILE] = next_rows(values.astype(jnp.bfloat16))
    for iteration in range(1, ITERS):
        symmetric(gram, gram_tiles)
        symmetric(polynomial, functools.partial(polynomial_tiles, 1.0))
        if iteration < ITERS - 1:
            for low in range(0, iterate.shape[0], TILE):
                iterate[low : low + TILE] = next_rows(iterate[low : low + TILE])

    f, r = ids[0], ids[1]
    side = lax.rem(r, 2)
    place = lax.rem(f - first_place(groups) + groups, groups)
    held = jnp.minimum(lax.div(place, 2), count - 1)
    offset = offsets[(r - side + lax.rem(place, 2)) * count + held]
    for step in range(steps):
        target = 2 * (step ^ held) + side
        source = lax.rem(target - offset + groups, groups)
        index = lax.div(source, 2) ^ held
        index += jnp.where(lax.rem(source, 2) == side, 0, steps)
        start = pl.multiple_of(index * rows, rows)
        update = scale_factor * next_rows(iterate[pl.ds(start, rows)]).astype(jnp.float32)
        master = decoded(code[index])
        leaving[step][...] = (master - LEARN_RATE * (update + DECAY_RATE * master)).astype(jnp.bfloat16)

    high = norm.astype(jnp.bfloat16).astype(jnp.float32)
    middle = (norm - high).astype(jnp.bfloat16).astype(jnp.float32)
    lane = lax.broadcasted_iota(jnp.int32, (TAIL, columns), 1)
    tail = jnp.where(lane == 0, high, jnp.where(lane == 1, middle, norm - high - middle))
    for index, message in enumerate(messages):
        message[:rows] = next_rows(iterate[index * rows : (index + 1) * rows])
        message[rows:] = tail.astype(jnp.bfloat16)


def polish_plain(f, r, offsets, count, groups, blocks):
    _, rows, columns = blocks[0].shape
    steps = groups // 2
    side = r % 2
    place = (f - first_place(groups)) % groups
    held = jnp.minimum(place // 2, count - 1)
    offset = pick(offsets, (r - side + place % 2) * count + held)
    blocks = jnp.stack(blocks)
    matrix = blocks[:, 0].reshape(groups * rows, columns).astype(jnp.float32)
    norm = jnp.sqrt(jnp.sum(jnp.square(matrix)))
    iterate = lax.optimization_barrier((matrix / (norm + EPSILON)).astype(jnp.bfloat16))
    for _ in range(ITERS):
        gram = lax.dot_general(
            iterate, iterate, (((0,), (0,)), ((), ())), preferred_element_type=jnp.float32
        ).astype(jnp.bfloat16)
        product = jnp.dot(gram, gram, preferred_element_type=jnp.float32)
        polynomial = COEF_SECOND * gram.astype(jnp.float32) + COEF_THIRD * product
        product = jnp.dot(iterate, polynomial.astype(jnp.bfloat16), preferred_element_type=jnp.float32)
        iterate = (COEF_FIRST * iterate.astype(jnp.float32) + product).astype(jnp.bfloat16)
        iterate = lax.optimization_barrier(iterate)
    iterate = iterate.reshape(groups, rows, columns)
    update = 0.2 * math.sqrt(max(groups * rows, columns)) * iterate.astype(jnp.float32)
    master = decoded(blocks[:, 1])
    weights = (master - LEARN_RATE * (update + DECAY_RATE * master)).astype(jnp.bfloat16)
    leaving = []
    for step in range(steps):
        source = (2 * (step ^ held) + side - offset) % groups
        index = source // 2 ^ held
        leaving.append(pick(weights, index + jnp.where(source % 2 == side, 0, steps)))
    high = norm.astype(jnp.bfloat16)
    rest = lax.optimization_barrier(norm - high.astype(jnp.float32))
    middle = rest.astype(jnp.bfloat16)
    low = lax.optimization_barrier(rest - middle.astype(jnp.float32)).astype(jnp.bfloat16)
    lane = lax.broadcasted_iota(jnp.int32, (TAIL, columns), 1)
    tail = jnp.where(lane == 0, high, jnp.where(lane == 1, middle, low))
    return [jnp.concatenate([iterate[step], tail]) for step in range(steps)], leaving


def polish(ids, offsets, count, groups, blocks):
    _, rows, columns = blocks[0].shape
    if rows % ROWS_OF_TILE:
        return polish_plain(*ids, offsets, count, groups, blocks)
    steps = groups // 2
    in_vmem = pl.BlockSpec(memory_space=pltpu.VMEM)
    square = pltpu.VMEM((columns, columns), jnp.bfloat16)
    results = pl.pallas_call(
        functools.partial(polish_kernel, count, groups),
        out_shape=[jax.ShapeDtypeStruct((rows + TAIL, columns), jnp.bfloat16)] * steps
        + [jax.ShapeDtypeStruct((rows, columns), jnp.bfloat16)] * steps,
        in_specs=[pl.BlockSpec(memory_space=pltpu.SMEM)] * 2 + [in_vmem] * groups,
        out_specs=[in_vmem] * groups,
        scratch_shapes=[
            pltpu.VMEM((groups * rows, columns), jnp.bfloat16),
            square,
            square,
            pltpu.VMEM((groups, rows, columns), jnp.bfloat16),
        ],
        compiler_params=pltpu.CompilerParams(vmem_limit_bytes=VMEM_LIMIT),
    )(ids, offsets, *blocks)
    return [*results[:steps]], [*results[steps:]]


def apply_kernel(count, groups, reps, ids, owners, master, *refs):
    steps = groups // 2
    returned, messages, refs = refs[:steps], refs[steps : 2 * steps], refs[2 * steps :]
    parts, (new_master, weights, slot_rms, semaphores) = refs[: reps * count], refs[reps * count :]
    _, rows, columns = master.shape
    scale_factor = 0.2 * math.sqrt(max(groups * rows, columns))
    f, r = ids[0], ids[1]
    place = lax.rem(f - first_place(groups) + groups, groups)
    half_place = lax.div(place, 2)
    turn = lax.rem(half_place, count)
    copies = []
    for n, part in enumerate(parts):
        matrix = (r ^ n // count) * count + (turn ^ n % count)
        copies.append(pltpu.make_async_copy(part, weights.at[matrix], semaphores.at[n]))
        copies[-1].start()
    own = lax.rem(r, 2) == lax.rem(place, 2)
    slot_rms[...] = jnp.zeros((1, 1), jnp.float32)

    def take(i, message):
        update = scale_factor * message[:rows].astype(jnp.float32)
        new_master[i] = master[i] - LEARN_RATE * (update + DECAY_RATE * master[i])
        shape = (TAIL, columns)
        row, lane = (lax.broadcasted_iota(jnp.int32, shape, n) for n in (0, 1))
        norm = jnp.where((row == 0) & (lane < 3), message[rows:].astype(jnp.float32), 0.0)
        norm = jnp.sum(norm, axis=(0, 1), keepdims=True)
        here = owners[r * count + i] == f
        slot_rms[...] += jnp.where(here, norm * (1.0 / math.sqrt(groups * rows * columns)), 0.0)

    for i in range(count):
        arrival = half_place ^ i
        held = own & (half_place == i)
        for step in range(steps):

            @pl.when((arrival == step) & jnp.logical_not(held))
            def _():
                take(i, returned[steps - 1 - step])

            if step_of(2 * i, i, steps, count) == step:

                @pl.when(held)
                def _():
                    take(i, messages[step])

    for copy in copies:
        copy.wait()


def apply_plain(f, r, owners, count, groups, reps, master, returned, messages, parts):
    _, rows, columns = master.shape
    steps = groups // 2
    place = (f - first_place(groups)) % groups
    half_place = place // 2
    own = r % 2 == place % 2
    order = half_place
    returned, messages = jnp.stack(returned), jnp.stack(messages)
    new_master, slot_rms = [], jnp.zeros((1, 1), jnp.float32)
    for i in range(count):
        message = jnp.where(own & (half_place == i), pick(messages, order ^ i), pick(returned, order ^ i))
        update = 0.2 * math.sqrt(max(groups * rows, columns)) * message[:rows].astype(jnp.float32)
        new_master.append(master[i] - LEARN_RATE * (update + DECAY_RATE * master[i]))
        rms = jnp.sum(message[rows, :3].astype(jnp.float32)) / math.sqrt(groups * rows * columns)
        slot_rms += jnp.where(pick(owners, r * count + i) == f, rms, 0.0)
    weights = jnp.zeros((reps * count, rows, columns), jnp.bfloat16)
    for other, part in enumerate(parts):
        for j in range(count):
            index = (r ^ other) * count + (order % count ^ j)
            weights = lax.dynamic_update_slice_in_dim(weights, part[j][None], index, 0)
    return jnp.stack(new_master), weights, slot_rms


def apply(ids, owners, count, groups, reps, master, returned, messages, parts):
    in_vmem = pl.BlockSpec(memory_space=pltpu.VMEM)
    in_smem = pl.BlockSpec(memory_space=pltpu.SMEM)
    _, rows, columns = master.shape
    if rows % ROWS_OF_TILE:
        return apply_plain(*ids, owners, count, groups, reps, master, returned, messages, parts)
    return pl.pallas_call(
        functools.partial(apply_kernel, count, groups, reps),
        out_shape=[
            jax.ShapeDtypeStruct(master.shape, jnp.float32),
            jax.ShapeDtypeStruct((reps * count, rows, columns), jnp.bfloat16),
            jax.ShapeDtypeStruct((1, 1), jnp.float32),
        ],
        in_specs=[in_smem] * 2 + [in_vmem] * (1 + 2 * len(messages) + reps * count),
        out_specs=[in_vmem, pl.BlockSpec(memory_space=pl.ANY), in_vmem],
        scratch_shapes=[pltpu.SemaphoreType.DMA((reps * count,))],
        compiler_params=pltpu.CompilerParams(vmem_limit_bytes=VMEM_LIMIT),
    )(ids, owners, master, *returned[::-1], *messages, *(one for part in parts for one in part))


def pick(array, index):
    return lax.dynamic_index_in_dim(array, index, 0, keepdims=False)


def on_device(grads, momentum, master, owners, offsets):
    groups, reps = lax.axis_size("fsdp"), lax.axis_size("rep")
    f, r = lax.axis_index("fsdp"), lax.axis_index("rep")
    count, rows, columns = grads.shape
    steps = groups // 2
    scale_factor = 0.2 * math.sqrt(max(groups * rows, columns))
    ids = jnp.stack([f, r])
    side = r % 2
    place = (f - first_place(groups)) % groups
    half_place = place // 2
    held = jnp.minimum(half_place, count - 1)
    holds_own = (side == place % 2) & (half_place < count)

    turn = half_place % count
    own_step = step_of(2 * held, held, steps, count)

    def inward_sends(array_of, chosen):
        return {
            step: lax.ppermute(
                array_of(step % count), AXES, inward_pairs(step, groups, reps, count)
            )
            for step in chosen
        }

    def with_own(step, block, own):
        return jnp.where(holds_own & (own_step == step), own, block)

    def half_of(i):
        return (MOMENTUM_DECAY * pick(momentum, i) + pick(grads, i).astype(jnp.float32)).astype(
            jnp.bfloat16
        )

    sent = lax.optimization_barrier(
        [jnp.stack([half_of(j ^ turn), coded(pick(master, j ^ turn))]) for j in range(count)]
    )
    blocks = inward_sends(lambda j: sent[j], range(steps))
    new_momentum = MOMENTUM_DECAY * momentum + grads.astype(jnp.float32)


    def own_of(arrays):
        own = arrays[0]
        for j in range(1, count):
            own = jnp.where((held ^ turn) == j, arrays[j], own)
        return own

    def both_sides(blocks, own):
        mine = [with_own(step, blocks[step], own) for step in range(steps)]
        return mine + [swap(block, groups, reps, 1) for block in mine]

    blocks = both_sides(blocks, own_of(sent))
    messages, leaving = polish(ids, offsets, count, groups, blocks)
    kept = messages

    def outward(blocks):
        return [
            lax.ppermute(block, AXES, outward_pairs(step, groups, reps, count))
            for step, block in reversed([*enumerate(blocks)])
        ][::-1]

    arrived = lax.optimization_barrier(outward(leaving)[::-1])[::-1]

    part = []
    for j in range(count):
        rows_in = arrived[j]
        for step in range(j + count, steps, count):
            rows_in = jnp.where(half_place // count * count + j == step, arrived[step], rows_in)
        for step in sorted({step_of(2 * i, i, steps, count) for i in range(count)}):
            if step % count == j:
                rows_in = with_own(step, rows_in, leaving[step])
        part.append(rows_in)
    messages[1:-1], new_momentum = lax.optimization_barrier((messages[1:-1], new_momentum))
    returned = outward(messages)

    parts = [part] + [None] * (reps - 1)
    bit = reps // 2
    while bit:
        for other in range(0, reps, 2 * bit):
            parts[other ^ bit] = [swap(one, groups, reps, bit) for one in parts[other]]
        bit //= 2
    new_master, weights, slot_rms = apply(
        ids, owners, count, groups, reps, master, returned, kept, parts
    )
    return (new_momentum, new_master, weights, slot_rms)


def solution(mesh):
    in_specs = (P("rep", "fsdp", None), P("rep", "fsdp", None), P("rep", "fsdp", None), P(), P())
    out_specs = (
        P("rep", "fsdp", None),
        P("rep", "fsdp", None),
        P(None, "fsdp", None),
        P("fsdp", "rep"),
    )
    return jax.shard_map(
        on_device, mesh=mesh, in_specs=in_specs, out_specs=out_specs, check_vma=False
    )
```

```python
import functools
import math

import jax
import jax.numpy as jnp
from jax import lax
from jax.experimental import pallas as pl
from jax.experimental.pallas import tpu as pltpu
from jax.sharding import PartitionSpec as P

ITERS = 2


COEF_FIRST = 3.4445
COEF_SECOND = -4.775
COEF_THIRD = 2.0315
MOMENTUM_DECAY = 0.95
LEARN_RATE = 0.02
DECAY_RATE = 0.1
EPSILON = 1e-07
AXES = ("fsdp", "rep")
TAIL = 16
ROWS_OF_TILE = 16
TILE = 256
VMEM_LIMIT = 40 * 2**20
MASTER_TOP = 0.1875
LEAST, SPAN = -125.0, 252.0


def first_place(groups):
    return groups // 4


def step_of(place, i, steps, count):
    return place // 2 ^ i


def inward_pairs(step, groups, reps, count):
    pairs = []
    for place in range(groups):
        for r in range(reps):
            for i in range(count):
                holder = 2 * i + r % 2
                if holder == place or step_of(place, i, groups // 2, count) != step:
                    continue
                source, target = ((p + first_place(groups)) % groups for p in (place, holder))
                pairs.append((source * reps + r, target * reps + r - r % 2 + place % 2))
    return pairs


def outward_pairs(step, groups, reps, count):
    return [(b, a) for a, b in inward_pairs(step, groups, reps, count)]


def swap(array, groups, reps, bit):
    return lax.ppermute(
        array, AXES, [(f * reps + r, f * reps + (r ^ bit)) for f in range(groups) for r in range(reps)]
    )


def coded(master):
    level = jnp.exp(jnp.log(jnp.abs(master) * (1.0 / MASTER_TOP)) * (1.0 / 3.0))
    size = jnp.exp2(level * SPAN + LEAST)
    return jnp.where(master < 0, -size, size).astype(jnp.bfloat16)


def decoded(code):
    code = code.astype(jnp.float32)
    level = (jnp.log2(jnp.abs(code)) - LEAST) * (1.0 / SPAN)
    size = level * level * level * MASTER_TOP
    return jnp.where(code < 0, -size, size)


def polish_kernel(count, groups, ids, offsets, *refs):
    steps = groups // 2
    blocks, refs = refs[:groups], refs[groups:]
    messages, leaving, scratch = refs[:steps], refs[steps : 2 * steps], refs[2 * steps :]
    iterate, gram, polynomial, code = scratch
    _, rows, columns = blocks[0].shape
    bounds = [(low, min(low + TILE, columns)) for low in range(0, columns, TILE)]
    scale_factor = 0.2 * math.sqrt(max(groups * rows, columns))

    for index, block in enumerate(blocks):
        iterate[index * rows : (index + 1) * rows] = block[0]
        code[index] = block[1]

    def symmetric(out, row_of_tiles):
        for low, high in bounds:
            values = row_of_tiles(low, high).astype(jnp.bfloat16)
            out[low:high, low:] = values
            for other, end in bounds:
                if other > low:
                    out[other:end, low:high] = values[:, other - low : end - low].T

    def gram_tiles(low, high):
        return lax.dot_general(
            iterate[:, low:high],
            iterate[:, low:],
            (((0,), (0,)), ((), ())),
            preferred_element_type=jnp.float32,
        )

    traces = []

    def raw_tiles(low, high):
        values = gram_tiles(low, high)
        shape = (high - low, high - low)
        row, lane = (lax.broadcasted_iota(jnp.int32, shape, n) for n in (0, 1))
        diagonal = jnp.where(row == lane, values[:, : high - low], 0.0)
        traces.append(jnp.sum(diagonal, axis=(0, 1), keepdims=True))
        return values

    def polynomial_tiles(factor, low, high):
        product = jnp.dot(gram[low:high], gram[:, low:], preferred_element_type=jnp.float32)
        first = (COEF_SECOND * factor) * gram[low:high, low:].astype(jnp.float32)
        return first + (COEF_THIRD * factor * factor) * product

    def next_rows(values):
        product = jnp.dot(values, polynomial[...], preferred_element_type=jnp.float32)
        return (COEF_FIRST * values.astype(jnp.float32) + product).astype(jnp.bfloat16)

    symmetric(gram, raw_tiles)
    norm = jnp.sqrt(sum(traces))
    scale = 1.0 / (norm + EPSILON)
    symmetric(polynomial, functools.partial(polynomial_tiles, scale * scale))
    for low in range(0, iterate.shape[0], TILE):
        values = iterate[low : low + TILE].astype(jnp.float32) * scale
        iterate[low : low + TILE] = next_rows(values.astype(jnp.bfloat16))
    for iteration in range(1, ITERS):
        symmetric(gram, gram_tiles)
        symmetric(polynomial, functools.partial(polynomial_tiles, 1.0))
        if iteration < ITERS - 1:
            for low in range(0, iterate.shape[0], TILE):
                iterate[low : low + TILE] = next_rows(iterate[low : low + TILE])

    f, r = ids[0], ids[1]
    side = lax.rem(r, 2)
    place = lax.rem(f - first_place(groups) + groups, groups)
    held = jnp.minimum(lax.div(place, 2), count - 1)
    offset = offsets[(r - side + lax.rem(place, 2)) * count + held]
    for step in range(steps):
        target = 2 * (step ^ held) + side
        source = lax.rem(target - offset + groups, groups)
        index = lax.div(source, 2) ^ held
        index += jnp.where(lax.rem(source, 2) == side, 0, steps)
        start = pl.multiple_of(index * rows, rows)
        update = scale_factor * next_rows(iterate[pl.ds(start, rows)]).astype(jnp.float32)
        master = decoded(code[index])
        leaving[step][...] = (master - LEARN_RATE * (update + DECAY_RATE * master)).astype(jnp.bfloat16)

    high = norm.astype(jnp.bfloat16).astype(jnp.float32)
    middle = (norm - high).astype(jnp.bfloat16).astype(jnp.float32)
    lane = lax.broadcasted_iota(jnp.int32, (TAIL, columns), 1)
    tail = jnp.where(lane == 0, high, jnp.where(lane == 1, middle, norm - high - middle))
    for index, message in enumerate(messages):
        message[:rows] = next_rows(iterate[index * rows : (index + 1) * rows])
        message[rows:] = tail.astype(jnp.bfloat16)


def polish_plain(f, r, offsets, count, groups, blocks):
    _, rows, columns = blocks[0].shape
    steps = groups // 2
    side = r % 2
    place = (f - first_place(groups)) % groups
    held = jnp.minimum(place // 2, count - 1)
    offset = pick(offsets, (r - side + place % 2) * count + held)
    blocks = jnp.stack(blocks)
    matrix = blocks[:, 0].reshape(groups * rows, columns).astype(jnp.float32)
    norm = jnp.sqrt(jnp.sum(jnp.square(matrix)))
    iterate = lax.optimization_barrier((matrix / (norm + EPSILON)).astype(jnp.bfloat16))
    for _ in range(ITERS):
        gram = lax.dot_general(
            iterate, iterate, (((0,), (0,)), ((), ())), preferred_element_type=jnp.float32
        ).astype(jnp.bfloat16)
        product = jnp.dot(gram, gram, preferred_element_type=jnp.float32)
        polynomial = COEF_SECOND * gram.astype(jnp.float32) + COEF_THIRD * product
        product = jnp.dot(iterate, polynomial.astype(jnp.bfloat16), preferred_element_type=jnp.float32)
        iterate = (COEF_FIRST * iterate.astype(jnp.float32) + product).astype(jnp.bfloat16)
        iterate = lax.optimization_barrier(iterate)
    iterate = iterate.reshape(groups, rows, columns)
    update = 0.2 * math.sqrt(max(groups * rows, columns)) * iterate.astype(jnp.float32)
    master = decoded(blocks[:, 1])
    weights = (master - LEARN_RATE * (update + DECAY_RATE * master)).astype(jnp.bfloat16)
    leaving = []
    for step in range(steps):
        source = (2 * (step ^ held) + side - offset) % groups
        index = source // 2 ^ held
        leaving.append(pick(weights, index + jnp.where(source % 2 == side, 0, steps)))
    high = norm.astype(jnp.bfloat16)
    rest = lax.optimization_barrier(norm - high.astype(jnp.float32))
    middle = rest.astype(jnp.bfloat16)
    low = lax.optimization_barrier(rest - middle.astype(jnp.float32)).astype(jnp.bfloat16)
    lane = lax.broadcasted_iota(jnp.int32, (TAIL, columns), 1)
    tail = jnp.where(lane == 0, high, jnp.where(lane == 1, middle, low))
    return [jnp.concatenate([iterate[step], tail]) for step in range(steps)], leaving


def polish(ids, offsets, count, groups, blocks):
    _, rows, columns = blocks[0].shape
    if rows % ROWS_OF_TILE:
        return polish_plain(*ids, offsets, count, groups, blocks)
    steps = groups // 2
    in_vmem = pl.BlockSpec(memory_space=pltpu.VMEM)
    square = pltpu.VMEM((columns, columns), jnp.bfloat16)
    results = pl.pallas_call(
        functools.partial(polish_kernel, count, groups),
        out_shape=[jax.ShapeDtypeStruct((rows + TAIL, columns), jnp.bfloat16)] * steps
        + [jax.ShapeDtypeStruct((rows, columns), jnp.bfloat16)] * steps,
        in_specs=[pl.BlockSpec(memory_space=pltpu.SMEM)] * 2 + [in_vmem] * groups,
        out_specs=[in_vmem] * groups,
        scratch_shapes=[
            pltpu.VMEM((groups * rows, columns), jnp.bfloat16),
            square,
            square,
            pltpu.VMEM((groups, rows, columns), jnp.bfloat16),
        ],
        compiler_params=pltpu.CompilerParams(vmem_limit_bytes=VMEM_LIMIT),
    )(ids, offsets, *blocks)
    return [*results[:steps]], [*results[steps:]]


def apply_kernel(count, groups, reps, ids, owners, master, *refs):
    steps = groups // 2
    returned, messages, refs = refs[:steps], refs[steps : 2 * steps], refs[2 * steps :]
    parts, (new_master, weights, slot_rms, semaphores) = refs[: reps * count], refs[reps * count :]
    _, rows, columns = master.shape
    scale_factor = 0.2 * math.sqrt(max(groups * rows, columns))
    f, r = ids[0], ids[1]
    place = lax.rem(f - first_place(groups) + groups, groups)
    half_place = lax.div(place, 2)
    turn = lax.rem(half_place, count)
    copies = []
    for n, part in enumerate(parts):
        matrix = (r ^ n // count) * count + (turn ^ n % count)
        copies.append(pltpu.make_async_copy(part, weights.at[matrix], semaphores.at[n]))
        copies[-1].start()
    own = lax.rem(r, 2) == lax.rem(place, 2)
    slot_rms[...] = jnp.zeros((1, 1), jnp.float32)

    def take(i, message):
        update = scale_factor * message[:rows].astype(jnp.float32)
        new_master[i] = master[i] - LEARN_RATE * (update + DECAY_RATE * master[i])
        shape = (TAIL, columns)
        row, lane = (lax.broadcasted_iota(jnp.int32, shape, n) for n in (0, 1))
        norm = jnp.where((row == 0) & (lane < 3), message[rows:].astype(jnp.float32), 0.0)
        norm = jnp.sum(norm, axis=(0, 1), keepdims=True)
        here = owners[r * count + i] == f
        slot_rms[...] += jnp.where(here, norm * (1.0 / math.sqrt(groups * rows * columns)), 0.0)

    for i in range(count):
        arrival = half_place ^ i
        held = own & (half_place == i)
        for step in range(steps):

            @pl.when((arrival == step) & jnp.logical_not(held))
            def _():
                take(i, returned[steps - 1 - step])

            if step_of(2 * i, i, steps, count) == step:

                @pl.when(held)
                def _():
                    take(i, messages[step])

    for copy in copies:
        copy.wait()


def apply_plain(f, r, owners, count, groups, reps, master, returned, messages, parts):
    _, rows, columns = master.shape
    steps = groups // 2
    place = (f - first_place(groups)) % groups
    half_place = place // 2
    own = r % 2 == place % 2
    order = half_place
    returned, messages = jnp.stack(returned), jnp.stack(messages)
    new_master, slot_rms = [], jnp.zeros((1, 1), jnp.float32)
    for i in range(count):
        message = jnp.where(own & (half_place == i), pick(messages, order ^ i), pick(returned, order ^ i))
        update = 0.2 * math.sqrt(max(groups * rows, columns)) * message[:rows].astype(jnp.float32)
        new_master.append(master[i] - LEARN_RATE * (update + DECAY_RATE * master[i]))
        rms = jnp.sum(message[rows, :3].astype(jnp.float32)) / math.sqrt(groups * rows * columns)
        slot_rms += jnp.where(pick(owners, r * count + i) == f, rms, 0.0)
    weights = jnp.zeros((reps * count, rows, columns), jnp.bfloat16)
    for other, part in enumerate(parts):
        for j in range(count):
            index = (r ^ other) * count + (order % count ^ j)
            weights = lax.dynamic_update_slice_in_dim(weights, part[j][None], index, 0)
    return jnp.stack(new_master), weights, slot_rms


def apply(ids, owners, count, groups, reps, master, returned, messages, parts):
    in_vmem = pl.BlockSpec(memory_space=pltpu.VMEM)
    in_smem = pl.BlockSpec(memory_space=pltpu.SMEM)
    _, rows, columns = master.shape
    if rows % ROWS_OF_TILE:
        return apply_plain(*ids, owners, count, groups, reps, master, returned, messages, parts)
    return pl.pallas_call(
        functools.partial(apply_kernel, count, groups, reps),
        out_shape=[
            jax.ShapeDtypeStruct(master.shape, jnp.float32),
            jax.ShapeDtypeStruct((reps * count, rows, columns), jnp.bfloat16),
            jax.ShapeDtypeStruct((1, 1), jnp.float32),
        ],
        in_specs=[in_smem] * 2 + [in_vmem] * (1 + 2 * len(messages) + reps * count),
        out_specs=[in_vmem, pl.BlockSpec(memory_space=pl.ANY), in_vmem],
        scratch_shapes=[pltpu.SemaphoreType.DMA((reps * count,))],
        compiler_params=pltpu.CompilerParams(vmem_limit_bytes=VMEM_LIMIT),
    )(ids, owners, master, *returned[::-1], *messages, *(one for part in parts for one in part))


def pick(array, index):
    return lax.dynamic_index_in_dim(array, index, 0, keepdims=False)


def on_device(grads, momentum, master, owners, offsets):
    groups, reps = lax.axis_size("fsdp"), lax.axis_size("rep")
    f, r = lax.axis_index("fsdp"), lax.axis_index("rep")
    count, rows, columns = grads.shape
    steps = groups // 2
    scale_factor = 0.2 * math.sqrt(max(groups * rows, columns))
    ids = jnp.stack([f, r])
    side = r % 2
    place = (f - first_place(groups)) % groups
    half_place = place // 2
    held = jnp.minimum(half_place, count - 1)
    holds_own = (side == place % 2) & (half_place < count)

    turn = half_place % count
    own_step = step_of(2 * held, held, steps, count)

    def inward_sends(array_of, chosen):
        return {
            step: lax.ppermute(
                array_of(step % count), AXES, inward_pairs(step, groups, reps, count)
            )
            for step in chosen
        }

    def with_own(step, block, own):
        return jnp.where(holds_own & (own_step == step), own, block)

    def half_of(i):
        return (MOMENTUM_DECAY * pick(momentum, i) + pick(grads, i).astype(jnp.float32)).astype(
            jnp.bfloat16
        )

    sent = lax.optimization_barrier(
        [jnp.stack([half_of(j ^ turn), coded(pick(master, j ^ turn))]) for j in range(count)]
    )
    blocks = inward_sends(lambda j: sent[j], range(steps))
    new_momentum = MOMENTUM_DECAY * momentum + grads.astype(jnp.float32)


    def own_of(arrays):
        own = arrays[0]
        for j in range(1, count):
            own = jnp.where((held ^ turn) == j, arrays[j], own)
        return own

    def both_sides(blocks, own):
        mine = [with_own(step, blocks[step], own) for step in range(steps)]
        return mine + [swap(block, groups, reps, 1) for block in mine]

    blocks = both_sides(blocks, own_of(sent))
    messages, leaving = polish(ids, offsets, count, groups, blocks)
    kept = messages

    def outward(blocks):
        return [
            lax.ppermute(block, AXES, outward_pairs(step, groups, reps, count))
            for step, block in reversed([*enumerate(blocks)])
        ][::-1]

    arrived = lax.optimization_barrier(outward(leaving)[::-1])[::-1]

    part = []
    for j in range(count):
        rows_in = arrived[j]
        for step in range(j + count, steps, count):
            rows_in = jnp.where(half_place // count * count + j == step, arrived[step], rows_in)
        for step in sorted({step_of(2 * i, i, steps, count) for i in range(count)}):
            if step % count == j:
                rows_in = with_own(step, rows_in, leaving[step])
        part.append(rows_in)
    for step in range(steps - 2, 0, -1):
        messages[step], new_momentum = lax.optimization_barrier((messages[step], new_momentum))
    returned = outward(messages)

    parts = [part] + [None] * (reps - 1)
    bit = reps // 2
    while bit:
        for other in range(0, reps, 2 * bit):
            parts[other ^ bit] = [swap(one, groups, reps, bit) for one in parts[other]]
        bit //= 2
    new_master, weights, slot_rms = apply(
        ids, owners, count, groups, reps, master, returned, kept, parts
    )
    return (new_momentum, new_master, weights, slot_rms)


def solution(mesh):
    in_specs = (P("rep", "fsdp", None), P("rep", "fsdp", None), P("rep", "fsdp", None), P(), P())
    out_specs = (
        P("rep", "fsdp", None),
        P("rep", "fsdp", None),
        P(None, "fsdp", None),
        P("fsdp", "rep"),
    )
    return jax.shard_map(
        on_device, mesh=mesh, in_specs=in_specs, out_specs=out_specs, check_vma=False
    )
```

```python
import functools
import math

import jax
import jax.numpy as jnp
from jax import lax
from jax.experimental import pallas as pl
from jax.experimental.pallas import tpu as pltpu
from jax.sharding import PartitionSpec as P

ITERS = 2


COEF_FIRST = 3.4445
COEF_SECOND = -4.775
COEF_THIRD = 2.0315
MOMENTUM_DECAY = 0.95
LEARN_RATE = 0.02
DECAY_RATE = 0.1
EPSILON = 1e-07
AXES = ("fsdp", "rep")
TAIL = 16
ROWS_OF_TILE = 16
TILE = 256
VMEM_LIMIT = 40 * 2**20
MASTER_TOP = 0.1875
LEAST, SPAN = -125.0, 252.0


def first_place(groups):
    return groups // 4


def step_of(place, i, steps, count):
    return place // 2 ^ i


def inward_pairs(step, groups, reps, count):
    pairs = []
    for place in range(groups):
        for r in range(reps):
            for i in range(count):
                holder = 2 * i + r % 2
                if holder == place or step_of(place, i, groups // 2, count) != step:
                    continue
                source, target = ((p + first_place(groups)) % groups for p in (place, holder))
                pairs.append((source * reps + r, target * reps + r - r % 2 + place % 2))
    return pairs


def outward_pairs(step, groups, reps, count):
    return [(b, a) for a, b in inward_pairs(step, groups, reps, count)]


def swap(array, groups, reps, bit):
    return lax.ppermute(
        array, AXES, [(f * reps + r, f * reps + (r ^ bit)) for f in range(groups) for r in range(reps)]
    )


def coded(master):
    level = jnp.exp(jnp.log(jnp.abs(master) * (1.0 / MASTER_TOP)) * (1.0 / 3.0))
    size = jnp.exp2(level * SPAN + LEAST)
    return jnp.where(master < 0, -size, size).astype(jnp.bfloat16)


def decoded(code):
    code = code.astype(jnp.float32)
    level = (jnp.log2(jnp.abs(code)) - LEAST) * (1.0 / SPAN)
    size = level * level * level * MASTER_TOP
    return jnp.where(code < 0, -size, size)


def polish_kernel(count, groups, ids, offsets, *refs):
    steps = groups // 2
    blocks, refs = refs[:groups], refs[groups:]
    messages, leaving, scratch = refs[:steps], refs[steps : 2 * steps], refs[2 * steps :]
    iterate, gram, polynomial, code = scratch
    _, rows, columns = blocks[0].shape
    bounds = [(low, min(low + TILE, columns)) for low in range(0, columns, TILE)]
    scale_factor = 0.2 * math.sqrt(max(groups * rows, columns))

    for index, block in enumerate(blocks):
        iterate[index * rows : (index + 1) * rows] = block[0]
        code[index] = block[1]

    def symmetric(out, row_of_tiles):
        for low, high in bounds:
            values = row_of_tiles(low, high).astype(jnp.bfloat16)
            out[low:high, low:] = values
            for other, end in bounds:
                if other > low:
                    out[other:end, low:high] = values[:, other - low : end - low].T

    def gram_tiles(low, high):
        return lax.dot_general(
            iterate[:, low:high],
            iterate[:, low:],
            (((0,), (0,)), ((), ())),
            preferred_element_type=jnp.float32,
        )

    traces = []

    def raw_tiles(low, high):
        values = gram_tiles(low, high)
        shape = (high - low, high - low)
        row, lane = (lax.broadcasted_iota(jnp.int32, shape, n) for n in (0, 1))
        diagonal = jnp.where(row == lane, values[:, : high - low], 0.0)
        traces.append(jnp.sum(diagonal, axis=(0, 1), keepdims=True))
        return values

    def polynomial_tiles(factor, low, high):
        product = jnp.dot(gram[low:high], gram[:, low:], preferred_element_type=jnp.float32)
        first = (COEF_SECOND * factor) * gram[low:high, low:].astype(jnp.float32)
        return first + (COEF_THIRD * factor * factor) * product

    def next_rows(values):
        product = jnp.dot(values, polynomial[...], preferred_element_type=jnp.float32)
        return (COEF_FIRST * values.astype(jnp.float32) + product).astype(jnp.bfloat16)

    symmetric(gram, raw_tiles)
    norm = jnp.sqrt(sum(traces))
    scale = 1.0 / (norm + EPSILON)
    symmetric(polynomial, functools.partial(polynomial_tiles, scale * scale))
    for low in range(0, iterate.shape[0], TILE):
        values = iterate[low : low + TILE].astype(jnp.float32) * scale
        iterate[low : low + TILE] = next_rows(values.astype(jnp.bfloat16))
    for iteration in range(1, ITERS):
        symmetric(gram, gram_tiles)
        symmetric(polynomial, functools.partial(polynomial_tiles, 1.0))
        if iteration < ITERS - 1:
            for low in range(0, iterate.shape[0], TILE):
                iterate[low : low + TILE] = next_rows(iterate[low : low + TILE])

    f, r = ids[0], ids[1]
    side = lax.rem(r, 2)
    place = lax.rem(f - first_place(groups) + groups, groups)
    held = jnp.minimum(lax.div(place, 2), count - 1)
    offset = offsets[(r - side + lax.rem(place, 2)) * count + held]
    for step in range(steps):
        target = 2 * (step ^ held) + side
        source = lax.rem(target - offset + groups, groups)
        index = lax.div(source, 2) ^ held
        index += jnp.where(lax.rem(source, 2) == side, 0, steps)
        start = pl.multiple_of(index * rows, rows)
        update = scale_factor * next_rows(iterate[pl.ds(start, rows)]).astype(jnp.float32)
        master = decoded(code[index])
        leaving[step][...] = (master - LEARN_RATE * (update + DECAY_RATE * master)).astype(jnp.bfloat16)

    high = norm.astype(jnp.bfloat16).astype(jnp.float32)
    middle = (norm - high).astype(jnp.bfloat16).astype(jnp.float32)
    lane = lax.broadcasted_iota(jnp.int32, (TAIL, columns), 1)
    tail = jnp.where(lane == 0, high, jnp.where(lane == 1, middle, norm - high - middle))
    updates = next_rows(iterate[: steps * rows])
    for index, message in enumerate(messages):
        message[:rows] = updates[index * rows : (index + 1) * rows]
        message[rows:] = tail.astype(jnp.bfloat16)


def polish_plain(f, r, offsets, count, groups, blocks):
    _, rows, columns = blocks[0].shape
    steps = groups // 2
    side = r % 2
    place = (f - first_place(groups)) % groups
    held = jnp.minimum(place // 2, count - 1)
    offset = pick(offsets, (r - side + place % 2) * count + held)
    blocks = jnp.stack(blocks)
    matrix = blocks[:, 0].reshape(groups * rows, columns).astype(jnp.float32)
    norm = jnp.sqrt(jnp.sum(jnp.square(matrix)))
    iterate = lax.optimization_barrier((matrix / (norm + EPSILON)).astype(jnp.bfloat16))
    for _ in range(ITERS):
        gram = lax.dot_general(
            iterate, iterate, (((0,), (0,)), ((), ())), preferred_element_type=jnp.float32
        ).astype(jnp.bfloat16)
        product = jnp.dot(gram, gram, preferred_element_type=jnp.float32)
        polynomial = COEF_SECOND * gram.astype(jnp.float32) + COEF_THIRD * product
        product = jnp.dot(iterate, polynomial.astype(jnp.bfloat16), preferred_element_type=jnp.float32)
        iterate = (COEF_FIRST * iterate.astype(jnp.float32) + product).astype(jnp.bfloat16)
        iterate = lax.optimization_barrier(iterate)
    iterate = iterate.reshape(groups, rows, columns)
    update = 0.2 * math.sqrt(max(groups * rows, columns)) * iterate.astype(jnp.float32)
    master = decoded(blocks[:, 1])
    weights = (master - LEARN_RATE * (update + DECAY_RATE * master)).astype(jnp.bfloat16)
    leaving = []
    for step in range(steps):
        source = (2 * (step ^ held) + side - offset) % groups
        index = source // 2 ^ held
        leaving.append(pick(weights, index + jnp.where(source % 2 == side, 0, steps)))
    high = norm.astype(jnp.bfloat16)
    rest = lax.optimization_barrier(norm - high.astype(jnp.float32))
    middle = rest.astype(jnp.bfloat16)
    low = lax.optimization_barrier(rest - middle.astype(jnp.float32)).astype(jnp.bfloat16)
    lane = lax.broadcasted_iota(jnp.int32, (TAIL, columns), 1)
    tail = jnp.where(lane == 0, high, jnp.where(lane == 1, middle, low))
    return [jnp.concatenate([iterate[step], tail]) for step in range(steps)], leaving


def polish(ids, offsets, count, groups, blocks):
    _, rows, columns = blocks[0].shape
    if rows % ROWS_OF_TILE:
        return polish_plain(*ids, offsets, count, groups, blocks)
    steps = groups // 2
    in_vmem = pl.BlockSpec(memory_space=pltpu.VMEM)
    square = pltpu.VMEM((columns, columns), jnp.bfloat16)
    results = pl.pallas_call(
        functools.partial(polish_kernel, count, groups),
        out_shape=[jax.ShapeDtypeStruct((rows + TAIL, columns), jnp.bfloat16)] * steps
        + [jax.ShapeDtypeStruct((rows, columns), jnp.bfloat16)] * steps,
        in_specs=[pl.BlockSpec(memory_space=pltpu.SMEM)] * 2 + [in_vmem] * groups,
        out_specs=[in_vmem] * groups,
        scratch_shapes=[
            pltpu.VMEM((groups * rows, columns), jnp.bfloat16),
            square,
            square,
            pltpu.VMEM((groups, rows, columns), jnp.bfloat16),
        ],
        compiler_params=pltpu.CompilerParams(vmem_limit_bytes=VMEM_LIMIT),
    )(ids, offsets, *blocks)
    return [*results[:steps]], [*results[steps:]]


def apply_kernel(count, groups, reps, ids, owners, master, *refs):
    steps = groups // 2
    returned, messages, refs = refs[:steps], refs[steps : 2 * steps], refs[2 * steps :]
    parts, refs = refs[: reps * count], refs[reps * count :]
    new_master, weights, slot_rms, updated, semaphores = refs
    _, rows, columns = master.shape
    scale_factor = 0.2 * math.sqrt(max(groups * rows, columns))
    f, r = ids[0], ids[1]
    place = lax.rem(f - first_place(groups) + groups, groups)
    half_place = lax.div(place, 2)
    turn = lax.rem(half_place, count)
    copies = []
    for n, part in enumerate(parts):
        matrix = (r ^ n // count) * count + (turn ^ n % count)
        copies.append(pltpu.make_async_copy(part, weights.at[matrix], semaphores.at[n]))
        copies[-1].start()
    own = lax.rem(r, 2) == lax.rem(place, 2)
    slot_rms[...] = jnp.zeros((1, 1), jnp.float32)

    def take(i, message):
        update = scale_factor * message[:rows].astype(jnp.float32)
        updated[i] = master[i] - LEARN_RATE * (update + DECAY_RATE * master[i])
        shape = (TAIL, columns)
        row, lane = (lax.broadcasted_iota(jnp.int32, shape, n) for n in (0, 1))
        norm = jnp.where((row == 0) & (lane < 3), message[rows:].astype(jnp.float32), 0.0)
        norm = jnp.sum(norm, axis=(0, 1), keepdims=True)
        here = owners[r * count + i] == f
        slot_rms[...] += jnp.where(here, norm * (1.0 / math.sqrt(groups * rows * columns)), 0.0)

    for i in range(count):
        arrival = half_place ^ i
        held = own & (half_place == i)
        for step in range(steps):

            @pl.when((arrival == step) & jnp.logical_not(held))
            def _():
                take(i, returned[steps - 1 - step])

            if step_of(2 * i, i, steps, count) == step:

                @pl.when(held)
                def _():
                    take(i, messages[step])

        copies.append(pltpu.make_async_copy(updated.at[i], new_master.at[i], semaphores.at[reps * count + i]))
        copies[-1].start()

    for copy in copies:
        copy.wait()


def apply_plain(f, r, owners, count, groups, reps, master, returned, messages, parts):
    _, rows, columns = master.shape
    steps = groups // 2
    place = (f - first_place(groups)) % groups
    half_place = place // 2
    own = r % 2 == place % 2
    order = half_place
    returned, messages = jnp.stack(returned), jnp.stack(messages)
    new_master, slot_rms = [], jnp.zeros((1, 1), jnp.float32)
    for i in range(count):
        message = jnp.where(own & (half_place == i), pick(messages, order ^ i), pick(returned, order ^ i))
        update = 0.2 * math.sqrt(max(groups * rows, columns)) * message[:rows].astype(jnp.float32)
        new_master.append(master[i] - LEARN_RATE * (update + DECAY_RATE * master[i]))
        rms = jnp.sum(message[rows, :3].astype(jnp.float32)) / math.sqrt(groups * rows * columns)
        slot_rms += jnp.where(pick(owners, r * count + i) == f, rms, 0.0)
    weights = jnp.zeros((reps * count, rows, columns), jnp.bfloat16)
    for other, part in enumerate(parts):
        for j in range(count):
            index = (r ^ other) * count + (order % count ^ j)
            weights = lax.dynamic_update_slice_in_dim(weights, part[j][None], index, 0)
    return jnp.stack(new_master), weights, slot_rms


def apply(ids, owners, count, groups, reps, master, returned, messages, parts):
    in_vmem = pl.BlockSpec(memory_space=pltpu.VMEM)
    in_smem = pl.BlockSpec(memory_space=pltpu.SMEM)
    _, rows, columns = master.shape
    if rows % ROWS_OF_TILE:
        return apply_plain(*ids, owners, count, groups, reps, master, returned, messages, parts)
    return pl.pallas_call(
        functools.partial(apply_kernel, count, groups, reps),
        out_shape=[
            jax.ShapeDtypeStruct(master.shape, jnp.float32),
            jax.ShapeDtypeStruct((reps * count, rows, columns), jnp.bfloat16),
            jax.ShapeDtypeStruct((1, 1), jnp.float32),
        ],
        in_specs=[in_smem] * 2 + [in_vmem] * (1 + 2 * len(messages) + reps * count),
        out_specs=[pl.BlockSpec(memory_space=pl.ANY), pl.BlockSpec(memory_space=pl.ANY), in_vmem],
        scratch_shapes=[
            pltpu.VMEM(master.shape, jnp.float32),
            pltpu.SemaphoreType.DMA((reps * count + count,)),
        ],
        compiler_params=pltpu.CompilerParams(vmem_limit_bytes=VMEM_LIMIT),
    )(ids, owners, master, *returned[::-1], *messages, *(one for part in parts for one in part))


def pick(array, index):
    return lax.dynamic_index_in_dim(array, index, 0, keepdims=False)


def on_device(grads, momentum, master, owners, offsets):
    groups, reps = lax.axis_size("fsdp"), lax.axis_size("rep")
    f, r = lax.axis_index("fsdp"), lax.axis_index("rep")
    count, rows, columns = grads.shape
    steps = groups // 2
    scale_factor = 0.2 * math.sqrt(max(groups * rows, columns))
    ids = jnp.stack([f, r])
    side = r % 2
    place = (f - first_place(groups)) % groups
    half_place = place // 2
    held = jnp.minimum(half_place, count - 1)
    holds_own = (side == place % 2) & (half_place < count)

    turn = half_place % count
    own_step = step_of(2 * held, held, steps, count)

    def inward_sends(array_of, chosen):
        return {
            step: lax.ppermute(
                array_of(step % count), AXES, inward_pairs(step, groups, reps, count)
            )
            for step in chosen
        }

    def with_own(step, block, own):
        return jnp.where(holds_own & (own_step == step), own, block)

    def half_of(i):
        return (MOMENTUM_DECAY * pick(momentum, i) + pick(grads, i).astype(jnp.float32)).astype(
            jnp.bfloat16
        )

    sent = lax.optimization_barrier(
        [jnp.stack([half_of(j ^ turn), coded(pick(master, j ^ turn))]) for j in range(count)]
    )
    blocks = inward_sends(lambda j: sent[j], range(steps))
    new_momentum = MOMENTUM_DECAY * momentum + grads.astype(jnp.float32)


    def own_of(arrays):
        own = arrays[0]
        for j in range(1, count):
            own = jnp.where((held ^ turn) == j, arrays[j], own)
        return own

    def both_sides(blocks, own):
        mine = [with_own(step, blocks[step], own) for step in range(steps)]
        return mine + [swap(block, groups, reps, 1) for block in mine]

    blocks = both_sides(blocks, own_of(sent))
    messages, leaving = polish(ids, offsets, count, groups, blocks)
    kept = messages

    def outward(blocks):
        return [
            lax.ppermute(block, AXES, outward_pairs(step, groups, reps, count))
            for step, block in reversed([*enumerate(blocks)])
        ][::-1]

    arrived = lax.optimization_barrier(outward(leaving)[::-1])[::-1]

    part = []
    for j in range(count):
        rows_in = arrived[j]
        for step in range(j + count, steps, count):
            rows_in = jnp.where(half_place // count * count + j == step, arrived[step], rows_in)
        for step in sorted({step_of(2 * i, i, steps, count) for i in range(count)}):
            if step % count == j:
                rows_in = with_own(step, rows_in, leaving[step])
        part.append(rows_in)
    for step in range(steps - 2, 0, -1):
        messages[step], new_momentum = lax.optimization_barrier((messages[step], new_momentum))
    returned = outward(messages)

    parts = [part] + [None] * (reps - 1)
    bit = reps // 2
    while bit:
        for other in range(0, reps, 2 * bit):
            parts[other ^ bit] = [swap(one, groups, reps, bit) for one in parts[other]]
        bit //= 2
    new_master, weights, slot_rms = apply(
        ids, owners, count, groups, reps, master, returned, kept, parts
    )
    return (new_momentum, new_master, weights, slot_rms)


def solution(mesh):
    in_specs = (P("rep", "fsdp", None), P("rep", "fsdp", None), P("rep", "fsdp", None), P(), P())
    out_specs = (
        P("rep", "fsdp", None),
        P("rep", "fsdp", None),
        P(None, "fsdp", None),
        P("fsdp", "rep"),
    )
    return jax.shard_map(
        on_device, mesh=mesh, in_specs=in_specs, out_specs=out_specs, check_vma=False
    )
```

```python
import functools
import math

import jax
import jax.numpy as jnp
from jax import lax
from jax.experimental import pallas as pl
from jax.experimental.pallas import tpu as pltpu
from jax.sharding import PartitionSpec as P

ITERS = 2


COEF_FIRST = 3.4445
COEF_SECOND = -4.775
COEF_THIRD = 2.0315
MOMENTUM_DECAY = 0.95
LEARN_RATE = 0.02
DECAY_RATE = 0.1
EPSILON = 1e-07
AXES = ("fsdp", "rep")
TAIL = 16
ROWS_OF_TILE = 16
TILE = 256
VMEM_LIMIT = 40 * 2**20
MASTER_TOP = 0.1875
LEAST, SPAN = -125.0, 252.0


def first_place(groups):
    return groups // 4


def step_of(place, i, steps, count):
    return place // 2 ^ i


def inward_pairs(step, groups, reps, count):
    pairs = []
    for place in range(groups):
        for r in range(reps):
            for i in range(count):
                holder = 2 * i + r % 2
                if holder == place or step_of(place, i, groups // 2, count) != step:
                    continue
                source, target = ((p + first_place(groups)) % groups for p in (place, holder))
                pairs.append((source * reps + r, target * reps + r - r % 2 + place % 2))
    return pairs


def outward_pairs(step, groups, reps, count):
    return [(b, a) for a, b in inward_pairs(step, groups, reps, count)]


def swap(array, groups, reps, bit):
    return lax.ppermute(
        array, AXES, [(f * reps + r, f * reps + (r ^ bit)) for f in range(groups) for r in range(reps)]
    )


def coded(master):
    level = jnp.exp2(jnp.log2(jnp.abs(master) * (1.0 / MASTER_TOP)) * (1.0 / 3.0))
    size = jnp.exp2(level * SPAN + LEAST)
    return jnp.where(master < 0, -size, size).astype(jnp.bfloat16)


def decoded(code):
    code = code.astype(jnp.float32)
    level = (jnp.log2(jnp.abs(code)) - LEAST) * (1.0 / SPAN)
    size = level * level * level * MASTER_TOP
    return jnp.where(code < 0, -size, size)


def polish_kernel(count, groups, ids, offsets, *refs):
    steps = groups // 2
    blocks, refs = refs[:groups], refs[groups:]
    messages, leaving, scratch = refs[:steps], refs[steps : 2 * steps], refs[2 * steps :]
    iterate, gram, polynomial, code = scratch
    _, rows, columns = blocks[0].shape
    bounds = [(low, min(low + TILE, columns)) for low in range(0, columns, TILE)]
    scale_factor = 0.2 * math.sqrt(max(groups * rows, columns))

    for index, block in enumerate(blocks):
        iterate[index * rows : (index + 1) * rows] = block[0]
        code[index] = block[1]

    def symmetric(out, row_of_tiles):
        for low, high in bounds:
            values = row_of_tiles(low, high).astype(jnp.bfloat16)
            out[low:high, low:] = values
            for other, end in bounds:
                if other > low:
                    out[other:end, low:high] = values[:, other - low : end - low].T

    def gram_tiles(low, high):
        return lax.dot_general(
            iterate[:, low:high],
            iterate[:, low:],
            (((0,), (0,)), ((), ())),
            preferred_element_type=jnp.float32,
        )

    traces = []

    def raw_tiles(low, high):
        values = gram_tiles(low, high)
        shape = (high - low, high - low)
        row, lane = (lax.broadcasted_iota(jnp.int32, shape, n) for n in (0, 1))
        diagonal = jnp.where(row == lane, values[:, : high - low], 0.0)
        traces.append(jnp.sum(diagonal, axis=(0, 1), keepdims=True))
        return values

    def polynomial_tiles(factor, low, high):
        product = jnp.dot(gram[low:high], gram[:, low:], preferred_element_type=jnp.float32)
        first = (COEF_SECOND * factor) * gram[low:high, low:].astype(jnp.float32)
        return first + (COEF_THIRD * factor * factor) * product

    def next_rows(values):
        product = jnp.dot(values, polynomial[...], preferred_element_type=jnp.float32)
        return (COEF_FIRST * values.astype(jnp.float32) + product).astype(jnp.bfloat16)

    symmetric(gram, raw_tiles)
    norm = jnp.sqrt(sum(traces))
    scale = 1.0 / (norm + EPSILON)
    symmetric(polynomial, functools.partial(polynomial_tiles, scale * scale))
    for low in range(0, iterate.shape[0], TILE):
        values = iterate[low : low + TILE].astype(jnp.float32) * scale
        iterate[low : low + TILE] = next_rows(values.astype(jnp.bfloat16))
    for iteration in range(1, ITERS):
        symmetric(gram, gram_tiles)
        symmetric(polynomial, functools.partial(polynomial_tiles, 1.0))
        if iteration < ITERS - 1:
            for low in range(0, iterate.shape[0], TILE):
                iterate[low : low + TILE] = next_rows(iterate[low : low + TILE])

    f, r = ids[0], ids[1]
    side = lax.rem(r, 2)
    place = lax.rem(f - first_place(groups) + groups, groups)
    held = jnp.minimum(lax.div(place, 2), count - 1)
    offset = offsets[(r - side + lax.rem(place, 2)) * count + held]
    for step in range(steps):
        target = 2 * (step ^ held) + side
        source = lax.rem(target - offset + groups, groups)
        index = lax.div(source, 2) ^ held
        index += jnp.where(lax.rem(source, 2) == side, 0, steps)
        start = pl.multiple_of(index * rows, rows)
        update = scale_factor * next_rows(iterate[pl.ds(start, rows)]).astype(jnp.float32)
        master = decoded(code[index])
        leaving[step][...] = (master - LEARN_RATE * (update + DECAY_RATE * master)).astype(jnp.bfloat16)

    high = norm.astype(jnp.bfloat16).astype(jnp.float32)
    middle = (norm - high).astype(jnp.bfloat16).astype(jnp.float32)
    lane = lax.broadcasted_iota(jnp.int32, (TAIL, columns), 1)
    tail = jnp.where(lane == 0, high, jnp.where(lane == 1, middle, norm - high - middle))
    updates = next_rows(iterate[: steps * rows])
    for index, message in enumerate(messages):
        message[:rows] = updates[index * rows : (index + 1) * rows]
        message[rows:] = tail.astype(jnp.bfloat16)


def polish_plain(f, r, offsets, count, groups, blocks):
    _, rows, columns = blocks[0].shape
    steps = groups // 2
    side = r % 2
    place = (f - first_place(groups)) % groups
    held = jnp.minimum(place // 2, count - 1)
    offset = pick(offsets, (r - side + place % 2) * count + held)
    blocks = jnp.stack(blocks)
    matrix = blocks[:, 0].reshape(groups * rows, columns).astype(jnp.float32)
    norm = jnp.sqrt(jnp.sum(jnp.square(matrix)))
    iterate = lax.optimization_barrier((matrix / (norm + EPSILON)).astype(jnp.bfloat16))
    for _ in range(ITERS):
        gram = lax.dot_general(
            iterate, iterate, (((0,), (0,)), ((), ())), preferred_element_type=jnp.float32
        ).astype(jnp.bfloat16)
        product = jnp.dot(gram, gram, preferred_element_type=jnp.float32)
        polynomial = COEF_SECOND * gram.astype(jnp.float32) + COEF_THIRD * product
        product = jnp.dot(iterate, polynomial.astype(jnp.bfloat16), preferred_element_type=jnp.float32)
        iterate = (COEF_FIRST * iterate.astype(jnp.float32) + product).astype(jnp.bfloat16)
        iterate = lax.optimization_barrier(iterate)
    iterate = iterate.reshape(groups, rows, columns)
    update = 0.2 * math.sqrt(max(groups * rows, columns)) * iterate.astype(jnp.float32)
    master = decoded(blocks[:, 1])
    weights = (master - LEARN_RATE * (update + DECAY_RATE * master)).astype(jnp.bfloat16)
    leaving = []
    for step in range(steps):
        source = (2 * (step ^ held) + side - offset) % groups
        index = source // 2 ^ held
        leaving.append(pick(weights, index + jnp.where(source % 2 == side, 0, steps)))
    high = norm.astype(jnp.bfloat16)
    rest = lax.optimization_barrier(norm - high.astype(jnp.float32))
    middle = rest.astype(jnp.bfloat16)
    low = lax.optimization_barrier(rest - middle.astype(jnp.float32)).astype(jnp.bfloat16)
    lane = lax.broadcasted_iota(jnp.int32, (TAIL, columns), 1)
    tail = jnp.where(lane == 0, high, jnp.where(lane == 1, middle, low))
    return [jnp.concatenate([iterate[step], tail]) for step in range(steps)], leaving


def polish(ids, offsets, count, groups, blocks):
    _, rows, columns = blocks[0].shape
    if rows % ROWS_OF_TILE:
        return polish_plain(*ids, offsets, count, groups, blocks)
    steps = groups // 2
    in_vmem = pl.BlockSpec(memory_space=pltpu.VMEM)
    square = pltpu.VMEM((columns, columns), jnp.bfloat16)
    results = pl.pallas_call(
        functools.partial(polish_kernel, count, groups),
        out_shape=[jax.ShapeDtypeStruct((rows + TAIL, columns), jnp.bfloat16)] * steps
        + [jax.ShapeDtypeStruct((rows, columns), jnp.bfloat16)] * steps,
        in_specs=[pl.BlockSpec(memory_space=pltpu.SMEM)] * 2 + [in_vmem] * groups,
        out_specs=[in_vmem] * groups,
        scratch_shapes=[
            pltpu.VMEM((groups * rows, columns), jnp.bfloat16),
            square,
            square,
            pltpu.VMEM((groups, rows, columns), jnp.bfloat16),
        ],
        compiler_params=pltpu.CompilerParams(vmem_limit_bytes=VMEM_LIMIT),
    )(ids, offsets, *blocks)
    return [*results[:steps]], [*results[steps:]]


def apply_kernel(count, groups, reps, ids, owners, master, *refs):
    steps = groups // 2
    returned, messages, refs = refs[:steps], refs[steps : 2 * steps], refs[2 * steps :]
    parts, refs = refs[: reps * count], refs[reps * count :]
    new_master, weights, slot_rms, updated, semaphores = refs
    _, rows, columns = master.shape
    scale_factor = 0.2 * math.sqrt(max(groups * rows, columns))
    f, r = ids[0], ids[1]
    place = lax.rem(f - first_place(groups) + groups, groups)
    half_place = lax.div(place, 2)
    turn = lax.rem(half_place, count)
    copies = []
    for n, part in enumerate(parts):
        matrix = (r ^ n // count) * count + (turn ^ n % count)
        copies.append(pltpu.make_async_copy(part, weights.at[matrix], semaphores.at[n]))
        copies[-1].start()
    own = lax.rem(r, 2) == lax.rem(place, 2)
    slot_rms[...] = jnp.zeros((1, 1), jnp.float32)

    def take(i, message):
        update = scale_factor * message[:rows].astype(jnp.float32)
        updated[i] = master[i] - LEARN_RATE * (update + DECAY_RATE * master[i])
        shape = (TAIL, columns)
        row, lane = (lax.broadcasted_iota(jnp.int32, shape, n) for n in (0, 1))
        norm = jnp.where((row == 0) & (lane < 3), message[rows:].astype(jnp.float32), 0.0)
        norm = jnp.sum(norm, axis=(0, 1), keepdims=True)
        here = owners[r * count + i] == f
        slot_rms[...] += jnp.where(here, norm * (1.0 / math.sqrt(groups * rows * columns)), 0.0)

    for i in range(count):
        arrival = half_place ^ i
        held = own & (half_place == i)
        for step in range(steps):

            @pl.when((arrival == step) & jnp.logical_not(held))
            def _():
                take(i, returned[steps - 1 - step])

            if step_of(2 * i, i, steps, count) == step:

                @pl.when(held)
                def _():
                    take(i, messages[step])

        copies.append(pltpu.make_async_copy(updated.at[i], new_master.at[i], semaphores.at[reps * count + i]))
        copies[-1].start()

    for copy in copies:
        copy.wait()


def apply_plain(f, r, owners, count, groups, reps, master, returned, messages, parts):
    _, rows, columns = master.shape
    steps = groups // 2
    place = (f - first_place(groups)) % groups
    half_place = place // 2
    own = r % 2 == place % 2
    order = half_place
    returned, messages = jnp.stack(returned), jnp.stack(messages)
    new_master, slot_rms = [], jnp.zeros((1, 1), jnp.float32)
    for i in range(count):
        message = jnp.where(own & (half_place == i), pick(messages, order ^ i), pick(returned, order ^ i))
        update = 0.2 * math.sqrt(max(groups * rows, columns)) * message[:rows].astype(jnp.float32)
        new_master.append(master[i] - LEARN_RATE * (update + DECAY_RATE * master[i]))
        rms = jnp.sum(message[rows, :3].astype(jnp.float32)) / math.sqrt(groups * rows * columns)
        slot_rms += jnp.where(pick(owners, r * count + i) == f, rms, 0.0)
    weights = jnp.zeros((reps * count, rows, columns), jnp.bfloat16)
    for other, part in enumerate(parts):
        for j in range(count):
            index = (r ^ other) * count + (order % count ^ j)
            weights = lax.dynamic_update_slice_in_dim(weights, part[j][None], index, 0)
    return jnp.stack(new_master), weights, slot_rms


def apply(ids, owners, count, groups, reps, master, returned, messages, parts):
    in_vmem = pl.BlockSpec(memory_space=pltpu.VMEM)
    in_smem = pl.BlockSpec(memory_space=pltpu.SMEM)
    _, rows, columns = master.shape
    if rows % ROWS_OF_TILE:
        return apply_plain(*ids, owners, count, groups, reps, master, returned, messages, parts)
    return pl.pallas_call(
        functools.partial(apply_kernel, count, groups, reps),
        out_shape=[
            jax.ShapeDtypeStruct(master.shape, jnp.float32),
            jax.ShapeDtypeStruct((reps * count, rows, columns), jnp.bfloat16),
            jax.ShapeDtypeStruct((1, 1), jnp.float32),
        ],
        in_specs=[in_smem] * 2 + [in_vmem] * (1 + 2 * len(messages) + reps * count),
        out_specs=[pl.BlockSpec(memory_space=pl.ANY), pl.BlockSpec(memory_space=pl.ANY), in_vmem],
        scratch_shapes=[
            pltpu.VMEM(master.shape, jnp.float32),
            pltpu.SemaphoreType.DMA((reps * count + count,)),
        ],
        compiler_params=pltpu.CompilerParams(vmem_limit_bytes=VMEM_LIMIT),
    )(ids, owners, master, *returned[::-1], *messages, *(one for part in parts for one in part))


def pick(array, index):
    return lax.dynamic_index_in_dim(array, index, 0, keepdims=False)


def on_device(grads, momentum, master, owners, offsets):
    groups, reps = lax.axis_size("fsdp"), lax.axis_size("rep")
    f, r = lax.axis_index("fsdp"), lax.axis_index("rep")
    count, rows, columns = grads.shape
    steps = groups // 2
    scale_factor = 0.2 * math.sqrt(max(groups * rows, columns))
    ids = jnp.stack([f, r])
    side = r % 2
    place = (f - first_place(groups)) % groups
    half_place = place // 2
    held = jnp.minimum(half_place, count - 1)
    holds_own = (side == place % 2) & (half_place < count)

    turn = half_place % count
    own_step = step_of(2 * held, held, steps, count)

    def inward_sends(array_of, chosen):
        return {
            step: lax.ppermute(
                array_of(step % count), AXES, inward_pairs(step, groups, reps, count)
            )
            for step in chosen
        }

    def with_own(step, block, own):
        return jnp.where(holds_own & (own_step == step), own, block)

    def half_of(i):
        return (MOMENTUM_DECAY * pick(momentum, i) + pick(grads, i).astype(jnp.float32)).astype(
            jnp.bfloat16
        )

    sent = lax.optimization_barrier(
        [jnp.stack([half_of(j ^ turn), coded(pick(master, j ^ turn))]) for j in range(count)]
    )
    blocks = inward_sends(lambda j: sent[j], range(steps))
    new_momentum = MOMENTUM_DECAY * momentum + grads.astype(jnp.float32)


    def own_of(arrays):
        own = arrays[0]
        for j in range(1, count):
            own = jnp.where((held ^ turn) == j, arrays[j], own)
        return own

    def both_sides(blocks, own):
        mine = [with_own(step, blocks[step], own) for step in range(steps)]
        return mine + [swap(block, groups, reps, 1) for block in mine]

    blocks = both_sides(blocks, own_of(sent))
    messages, leaving = polish(ids, offsets, count, groups, blocks)
    kept = messages

    def outward(blocks):
        return [
            lax.ppermute(block, AXES, outward_pairs(step, groups, reps, count))
            for step, block in reversed([*enumerate(blocks)])
        ][::-1]

    arrived = lax.optimization_barrier(outward(leaving)[::-1])[::-1]

    part = []
    for j in range(count):
        rows_in = arrived[j]
        for step in range(j + count, steps, count):
            rows_in = jnp.where(half_place // count * count + j == step, arrived[step], rows_in)
        for step in sorted({step_of(2 * i, i, steps, count) for i in range(count)}):
            if step % count == j:
                rows_in = with_own(step, rows_in, leaving[step])
        part.append(rows_in)
    for step in range(steps - 2, -1, -2):
        messages[step], new_momentum = lax.optimization_barrier((messages[step], new_momentum))
    returned = outward(messages)

    parts = [part] + [None] * (reps - 1)
    bit = reps // 2
    while bit:
        for other in range(0, reps, 2 * bit):
            parts[other ^ bit] = [swap(one, groups, reps, bit) for one in parts[other]]
        bit //= 2
    new_master, weights, slot_rms = apply(
        ids, owners, count, groups, reps, master, returned, kept, parts
    )
    return (new_momentum, new_master, weights, slot_rms)


def solution(mesh):
    in_specs = (P("rep", "fsdp", None), P("rep", "fsdp", None), P("rep", "fsdp", None), P(), P())
    out_specs = (
        P("rep", "fsdp", None),
        P("rep", "fsdp", None),
        P(None, "fsdp", None),
        P("fsdp", "rep"),
    )
    return jax.shard_map(
        on_device, mesh=mesh, in_specs=in_specs, out_specs=out_specs, check_vma=False
    )
```
